128 devices in a mesh: dp: 32 (over x, y, z_hi), space: 4 (over z_lo, core).
Axes of the slice: x: 4, y: 4, z: 4 (z_hi: 2, z_lo: 2; z = z_hi * 2 + z_lo), core: 2. Of those that a mesh axis runs over, the one named last changes fastest.
Arguments:
- features: bfloat16 [32, 8, 512, 384], P('dp', 'space'), may hold values from -6 to 6
- cotangent: bfloat16 [32, 8, 512, 384], P('dp', 'space'), may hold values from -6 to 6
- weight: bfloat16 [10368, 384], P('dp'), may hold values from -0.0625 to 0.0625
- occupancy: int32 [32, 8, 512], P('dp'), may hold values from 0 to 1, as said below
- neighbours: int32 [32, 8, 27], P('dp'), may hold values from -1 to 7, as said below
- first_moment: float32 [10368, 384], P('dp', 'space'), may hold values from -6 to 6
- second_moment: float32 [10368, 384], P('dp', 'space'), may hold values from 0.01 to 4
Outputs:
- input_grad: bfloat16 [32, 8, 512, 384], P('dp', 'space')
- new_first: float32 [10368, 384], P('dp', 'space')
- new_second: float32 [10368, 384], P('dp', 'space')
The draws below stay inside these ranges and needn't reach their ends.
Inputs may be any that keep to these rules, and one draw needn't show every extreme that they name: `neighbours`: slots s * 2 to s * 2 + 1 of a window lie on index s of space. Exactly 4 slots of each window hold a block, slot 7 always among them, and in every window one index of space has all 2 of its slots holding one. For a slot holding a block, entry 13 is the slot itself and entry 9 e1 + 3 e2 + e3 is the slot of the block displaced by (e1 - 1, e2 - 1, e3 - 1) block widths, or -1 if no block lies there; the relation is symmetric and entries name only slots holding blocks. Every entry of an empty slot is -1. `occupancy`: zero in every slot that holds no block.
All inputs are finite; a program needn't handle non-finite values.
Results may differ from the reference program's by a relative error of at most 0.006.
Values may be sent and summed in bfloat16 or wider, within the bound.
A program may use at most 192 MiB of HBM per device.

```python
import math
import jax
import jax.numpy as jnp
from jax import lax

C = 384
CAP = 2
WINDOWS = 32
GROUP = 8
N_SPACE = 4


def window_layout(key):
    group_size = N_SPACE * CAP
    live_count = group_size // 2
    key_full, key_order = jax.random.split(key)
    full_device = jax.random.randint(key_full, (), 0, N_SPACE)
    priority = jax.random.permutation(key_order, group_size).astype(jnp.int32)
    slot_ids = jnp.arange(group_size, dtype=jnp.int32)
    scores = priority + group_size * (slot_ids // CAP == full_device).astype(jnp.int32) + 2 * group_size * (slot_ids == group_size - 1).astype(jnp.int32)
    slot_order = jnp.argsort(-scores).astype(jnp.int32)
    cell_ids = jnp.arange(live_count, dtype=jnp.int32)
    cell_x = cell_ids % 2
    cell_y = cell_ids // 2 % 2
    cell_z = cell_ids // 4
    codes = jnp.arange(27, dtype=jnp.int32)
    step_x = codes // 9 - 1
    step_y = codes // 3 % 3 - 1
    step_z = codes % 3 - 1
    near_x = cell_x[:, None] + step_x[None, :]
    near_y = cell_y[:, None] + step_y[None, :]
    near_z = cell_z[:, None] + step_z[None, :]
    inside = (near_x >= 0) & (near_x < 2) & (near_y >= 0) & (near_y < 2) & (near_z >= 0) & (near_z < live_count // 4)
    near_cell = jnp.clip(near_x + 2 * near_y + 4 * near_z, 0, live_count - 1)
    near_slot = jnp.where(inside, jnp.take(slot_order, near_cell), -1).astype(jnp.int32)
    tables = jnp.full((group_size, 27), -1, jnp.int32).at[slot_order[:live_count]].set(near_slot)
    return tables


def window_tables(key):
    return jax.vmap(lambda window_index: window_layout(jax.random.fold_in(key, window_index)))(jnp.arange(WINDOWS))


def draw_neighbours(key, part):
    return window_tables(jax.random.fold_in(key, 11))


def draw_occupancy(key, part):
    tables = window_tables(jax.random.fold_in(key, 11))
    present = tables[:, :, 13] >= 0
    key_dense, key_voxel = jax.random.split(jax.random.fold_in(key, 23))
    thresholds = jax.random.randint(key_dense, (WINDOWS, N_SPACE * CAP), 8, 33)
    voxel_draws = jax.random.randint(key_voxel, (WINDOWS, N_SPACE * CAP, 512), 0, 32)
    filled = (voxel_draws < thresholds[:, :, None]) & present[:, :, None]
    return filled.astype(jnp.int32)


def strengthened(values, own_key, source, target, parts, factor):
    owner, partner = [(jnp.arange(values.shape[axis_at]) // (values.shape[axis_at] // parts)).reshape([-1 if axis == axis_at else 1 for axis in range(values.ndim)]) for axis_at in (source, target)]
    chosen = jax.random.permutation(own_key, parts)[partner]
    strong = (owner == chosen) | (owner == (partner + parts // 2) % parts)
    return jnp.where(strong, factor * values, values)


def shard_levels(own_key, extent, cuts, smallest, high):
    level = 1.0
    for dim, shards_of in cuts:
        steps = jax.random.uniform(jax.random.fold_in(jax.random.fold_in(own_key, 6), dim), (shards_of,), jnp.float32, smallest / len(cuts), high / len(cuts))
        level = level * jnp.repeat(jnp.exp(steps), extent[dim] // shards_of).reshape((-1,) + (1,) * (len(extent) - 1 - dim))
    return level


def scatter_about(stream_key, shape, width, reach, shards=(), kind=jnp.bfloat16):
    factor_of = shard_levels(stream_key, shape, shards, -0.22, 0.18) if shards else 1.0
    result = jax.random.normal(stream_key, shape, jnp.float32) * width * factor_of
    return jnp.minimum(jnp.maximum(result, -reach), reach).astype(kind)


def heavy_noise(key, dims, width, reach, shards, heavy, held_as=jnp.bfloat16):
    values = width * jax.random.normal(key, dims, jnp.float32)
    if shards:
        values = values * shard_levels(key, dims, shards, -0.22, 0.18)
    return jnp.clip(strengthened(values, jax.random.fold_in(key, 3), *heavy), -reach, reach).astype(held_as)


def setup_inputs(seed: int = 0) -> dict:
    key_of = jax.random.split(jax.random.key(seed), 8)
    return {
        "features": heavy_noise(key_of[0], (WINDOWS, GROUP, 512, C), 1.0, 6.0, ((0, 32), (1, 4)), (0, 3, 32, 2.75)),
        "cotangent": heavy_noise(key_of[1], (WINDOWS, GROUP, 512, C), 1.0, 6.0, ((0, 32), (1, 4)), (1, 3, 4, 2.0)),
        "weight": scatter_about(key_of[2], (27 * C, C), (27 * C) ** -0.5, 0.0625, ((0, 32),)),
        "occupancy": draw_occupancy(jax.random.fold_in(key_of[7], 71), 0),
        "neighbours": draw_neighbours(jax.random.fold_in(key_of[7], 71), 0),
        "first_moment": scatter_about(key_of[5], (27 * C, C), 1.0, 6.0, ((0, 32), (1, 4)), jnp.float32),
        "second_moment": jnp.clip(jnp.exp(math.log(4.0) - 5.9914646 * jax.random.uniform(key_of[6], (27 * C, C), jnp.float32) ** shard_levels(key_of[6], (27 * C, C), ((0, 32), (1, 4)), -0.2, 0.2)), 0.01, 4.0),
    }


EDGE_SPANS = ((7, 8), (0, 8), (0, 1))


def build_region(lookup, neighbour_rows):
    slab_list = []
    for first_axis in range(3):
        planes = []
        for second_axis in range(3):
            pieces = []
            for third_axis in range(3):
                offset_code = 9 * first_axis + 3 * second_axis + third_axis
                span_one = EDGE_SPANS[first_axis]
                span_two = EDGE_SPANS[second_axis]
                span_three = EDGE_SPANS[third_axis]
                window_part = lookup[:, span_one[0]:span_one[1], span_two[0]:span_two[1], span_three[0]:span_three[1], :]
                pieces.append(jnp.take(window_part, neighbour_rows[:, offset_code], axis=0))
            planes.append(jnp.concatenate(pieces, axis=3))
        slab_list.append(jnp.concatenate(planes, axis=2))
    return jnp.concatenate(slab_list, axis=1)


def shifted(region, offset):
    first_axis = offset // 9
    second_axis = (offset // 3) % 3
    third_axis = offset % 3
    moved = region[:, first_axis:first_axis + 8, second_axis:second_axis + 8, third_axis:third_axis + 8, :]
    return moved.reshape(-1, region.shape[-1])


def reference(features, cotangent, weight, occupancy, neighbours, first_moment, second_moment):
    channels = features.shape[3]
    group_size = features.shape[1]
    weight_cube = weight.reshape(channels, 27, channels)
    flat_rows = group_size * 512

    def one_window(running, inputs):
        window_feat, window_cot, window_occ, window_links = inputs
        voxel_mask = window_occ.astype(jnp.float32)
        masked = window_feat * window_occ[:, :, None].astype(jnp.bfloat16)
        lookup = jnp.concatenate([masked.reshape(group_size, 8, 8, 8, channels), jnp.zeros((1, 8, 8, 8, channels), jnp.bfloat16)], axis=0)
        slot_links = jnp.where(window_links < 0, group_size, window_links).astype(jnp.int32)
        region = build_region(lookup, slot_links)
        pre = jnp.zeros((flat_rows, channels), jnp.float32)
        for offset in range(27):
            pre = pre + jnp.dot(shifted(region, offset), weight_cube[:, offset, :], preferred_element_type=jnp.float32)
        mask_rows = voxel_mask.reshape(flat_rows, 1)
        cot_rows = window_cot.reshape(flat_rows, channels).astype(jnp.float32)
        sigmoid_pre = jax.nn.sigmoid(pre)
        delta_rows = (cot_rows * mask_rows * sigmoid_pre * (1.0 + pre * (1.0 - sigmoid_pre))).astype(jnp.bfloat16)
        delta_lookup = jnp.concatenate([delta_rows.reshape(group_size, 8, 8, 8, channels), jnp.zeros((1, 8, 8, 8, channels), jnp.bfloat16)], axis=0)
        delta_region = build_region(delta_lookup, slot_links)
        back_rows = jnp.zeros((flat_rows, channels), jnp.float32)
        for offset in range(27):
            back_rows = back_rows + lax.dot_general(shifted(delta_region, 26 - offset), weight_cube[:, offset, :], (((1,), (1,)), ((), ())), preferred_element_type=jnp.float32)
        grad_rows = (cot_rows + mask_rows * back_rows).astype(jnp.bfloat16)
        kernel_terms = [lax.dot_general(shifted(region, offset), delta_rows, (((0,), (0,)), ((), ())), preferred_element_type=jnp.float32) for offset in range(27)]
        kernel_sum = jnp.stack(kernel_terms, axis=1).reshape(27 * channels, channels)
        return running + kernel_sum, grad_rows.reshape(group_size, 512, channels)

    weight_sum, input_grad = lax.scan(one_window, jnp.zeros((27 * channels, channels), jnp.float32), (features, cotangent, occupancy, neighbours))
    scaled_grad = weight_sum / 64.0
    new_first = 0.9 * first_moment + 0.1 * scaled_grad
    new_second = 0.999 * second_moment + 0.001 * scaled_grad * scaled_grad
    return input_grad, new_first, new_second
```

```python
import jax
import jax.numpy as jnp
from jax import lax
from jax.experimental import pallas as pl
from jax.experimental.pallas import tpu as pltpu
from jax.sharding import PartitionSpec as P

LIVE = 4
LANES = 128
CHUNK = 336
CUT = 176
MESH = pl.DeviceIdType.MESH
VMEM_BYTES = 58 * 1024 * 1024


def fill_regions(table, blocks, regions, live):
    channels = blocks.shape[-1]
    row = lax.broadcasted_iota(jnp.int32, (1, 8, channels), 1)

    def plane(step, carry):
        r = step // 10
        i = step % 10
        first = jnp.where(i == 0, 0, jnp.where(i == 9, 2, 1))
        source = (i + 7) % 8
        code = 9 * first
        for c in range(3):
            pieces = []
            for second, start, count in ((0, 7, 1), (1, 0, 8), (2, 0, 1)):
                where = pl.ds(source * 8 + start, count)
                values = blocks[table[r, code + 3 * second + 1], where]
                if c != 1:
                    edge = blocks[table[r, code + 3 * second + c], where]
                    values = jnp.where(row == (7 if c == 0 else 0), edge, values)
                    values = pltpu.roll(values, 1 if c == 0 else 7, 1)
                pieces.append(values)
            line = jnp.concatenate(pieces, axis=0)
            for b in range(3):
                regions[3 * b + c, r, i] = (
                    line[b : b + 8].reshape(64, channels).astype(jnp.bfloat16)
                )
        return carry

    lax.fori_loop(0, live * 10, plane, 0)


def shifted_rows(regions, block, k, channels):
    a, bc = k // 9, k % 9
    return regions[bc, block, a : a + 8].reshape(512, channels)


def forward_kernel(
    table, slots, feat, cot, parts, sums, delta, weight, blocks, regions, delta_t, stage
):
    live = slots.shape[0]
    channels = feat.shape[-1]
    for r in range(live):
        blocks[r] = feat[slots[r]].astype(jnp.float32).reshape(64, 8, channels)
    blocks[live] = jnp.zeros((64, 8, channels), jnp.float32)
    fill_regions(table, blocks, regions, live)

    rows_of = 27 * channels // 32
    for d in range(32):
        stage[rows_of * d : rows_of * d + CHUNK] = parts[d % 2, d // 8, d // 2 % 4].astype(
            jnp.float32
        )
    for k in range(27):
        weight[k * channels : (k + 1) * channels] = stage[
            pl.ds(k, channels, stride=27), :
        ].astype(jnp.bfloat16)

    def one_block(r, carry):
        pre = jnp.zeros((512, LANES), jnp.float32)
        for group in (range(g, min(g + 2, 27)) for g in range(0, 27, 2)):
            lhs = jnp.concatenate(
                [shifted_rows(regions, r, k, channels) for k in group], axis=1
            )
            rhs = weight[group[0] * channels : (group[-1] + 1) * channels]
            pre = pre + jnp.dot(lhs, rhs, preferred_element_type=jnp.float32)
        gate = jax.nn.sigmoid(pre)
        value = cot[slots[r]].astype(jnp.float32) * gate * (1.0 + pre * (1.0 - gate))
        delta[r] = value.astype(jnp.bfloat16)
        return carry

    lax.fori_loop(0, live, one_block, 0)
    for r in range(live):
        delta_t[:, r * 512 : (r + 1) * 512] = (
            delta[r].astype(jnp.float32).T.astype(jnp.bfloat16)
        )

    for k in range(27):
        rows = jnp.concatenate(
            [shifted_rows(regions, r, k, channels) for r in range(live)], axis=0
        )
        part = jnp.dot(delta_t[...], rows, preferred_element_type=jnp.float32)
        stage[pl.ds(k, channels, stride=27), :] = part.T
    for d in range(32):
        sums[d % 2, d // 8, d // 2 % 4] = stage[rows_of * d : rows_of * d + CHUNK].astype(
            jnp.bfloat16
        )


def backward_kernel(table, slots, delta, weight, back, blocks, regions):
    live = slots.shape[0]
    channels = back.shape[-1]
    for r in range(live):
        blocks[r] = delta[r].astype(jnp.float32).reshape(64, 8, LANES)
    blocks[live] = jnp.zeros((64, 8, LANES), jnp.float32)
    fill_regions(table, blocks, regions, live)
    back[...] = jnp.zeros(back.shape, back.dtype)

    def one_block(r, carry):
        total = jnp.zeros((512, channels), jnp.float32)
        for group in (range(g, min(g + 4, 27)) for g in range(0, 27, 4)):
            lhs = jnp.concatenate(
                [shifted_rows(regions, r, 26 - k, LANES) for k in group], axis=1
            )
            rhs = jnp.concatenate(
                [weight[k * channels : (k + 1) * channels] for k in group], axis=1
            )
            total = total + lax.dot_general(
                lhs, rhs, (((1,), (1,)), ((), ())), preferred_element_type=jnp.float32
            )
        back[slots[r]] = total.astype(jnp.bfloat16)
        return carry

    lax.fori_loop(0, live, one_block, 0)


SMEM_SPEC = pl.BlockSpec(memory_space=pltpu.SMEM)
VMEM_SPEC = pl.BlockSpec(memory_space=pltpu.VMEM)


def forward_call(table, slots, feat, cot, parts):
    live, channels = slots.shape[0], feat.shape[-1]
    flops = 2 * 2 * live * 512 * 27 * channels * LANES
    return pl.pallas_call(
        forward_kernel,
        out_shape=(
            jax.ShapeDtypeStruct((2, 4, 4, CHUNK, LANES), jnp.bfloat16),
            jax.ShapeDtypeStruct((live, 512, LANES), jnp.bfloat16),
            jax.ShapeDtypeStruct((27 * channels, LANES), jnp.bfloat16),
        ),
        in_specs=[SMEM_SPEC] * 2 + [VMEM_SPEC] * 3,
        out_specs=(VMEM_SPEC,) * 3,
        scratch_shapes=[
            pltpu.VMEM((live + 1, 64, 8, channels), jnp.float32),
            pltpu.VMEM((9, live, 10, 64, channels), jnp.bfloat16),
            pltpu.VMEM((LANES, live * 512), jnp.bfloat16),
            pltpu.VMEM((27 * channels + 16, LANES), jnp.float32),
        ],
        compiler_params=pltpu.CompilerParams(vmem_limit_bytes=VMEM_BYTES),
        cost_estimate=pl.CostEstimate(flops=flops, bytes_accessed=10**7, transcendentals=10**6),
    )(table, slots, feat, cot, parts)


class Wires:
    def __init__(self, send_sem, recv_sem):
        self.send_sem, self.recv_sem = send_sem, recv_sem
        dp, space = lax.axis_index("dp"), lax.axis_index("space")
        self.x, self.y, self.z = dp // 8, dp // 2 % 4, dp % 2
        self.chip, self.core = space // 2, space % 2
        self.started = []
        self.count = 0

    def at(self, x=None, y=None, z=None, chip=None, core=None):
        x, y, z = self.x if x is None else x, self.y if y is None else y, self.z if z is None else z
        chip, core = self.chip if chip is None else chip, self.core if core is None else core
        return (x * 8 + y * 2 + z, chip * 2 + core)

    def step(self, axis, by):
        return self.at(**{axis: (getattr(self, axis) + by) % 4})

    def meet(self, others):
        barrier = pltpu.get_barrier_semaphore()
        for other in others:
            pl.semaphore_signal(barrier, inc=1, device_id=other, device_id_type=MESH)
        pl.semaphore_wait(barrier, len(others))

    def everyone(self):
        return (
            [self.step(axis, by) for axis in ("x", "y") for by in (1, 3)]
            + [self.at(z=1 - self.z), self.at(chip=1 - self.chip), self.at(core=1 - self.core)]
            + [self.at(chip=1 - self.chip, core=1 - self.core)]
        )

    def ticket(self):
        self.count += 1
        return self.count - 1

    def send(self, ticket, source, target, other):
        copy = pltpu.make_async_remote_copy(
            source,
            target,
            self.send_sem.at[ticket],
            self.recv_sem.at[ticket],
            device_id=other,
            device_id_type=MESH,
        )
        copy.start()
        self.started.append(copy)

    def arrived(self, ticket, landing):
        pltpu.make_async_remote_copy(
            landing,
            landing,
            self.send_sem.at[ticket],
            self.recv_sem.at[ticket],
            device_id=self.at(core=1 - self.core),
            device_id_type=MESH,
        ).wait_recv()

    def finish(self):
        for copy in self.started:
            copy.wait_send()


class RingGather:
    def __init__(self, wires, axis, block):
        self.wires, self.axis, self.block = wires, axis, block
        self.q = getattr(wires, axis)
        self.tickets = [wires.ticket() for _ in range(6)]

    def start(self):
        t, q = self.tickets, self.q
        right, left = self.wires.step(self.axis, 1), self.wires.step(self.axis, 3)
        for ticket, half, other in ((t[0], 0, right), (t[1], 1, left), (t[2], 1, right), (t[3], 0, left)):
            mine = self.block(q, half)
            self.wires.send(ticket, mine, mine, other)

    def forward(self):
        t, q = self.tickets, self.q
        right, left = self.wires.step(self.axis, 1), self.wires.step(self.axis, 3)
        for ticket, into, half, source, other in (
            (t[0], t[4], 0, (q + 3) % 4, right),
            (t[1], t[5], 1, (q + 1) % 4, left),
        ):
            piece = self.block(source, half)
            self.wires.arrived(ticket, piece)
            self.wires.send(into, piece, piece, other)

    def end(self):
        t, q = self.tickets, self.q
        self.wires.arrived(t[2], self.block((q + 3) % 4, 1))
        self.wires.arrived(t[3], self.block((q + 1) % 4, 0))
        self.wires.arrived(t[4], self.block((q + 2) % 4, 0))
        self.wires.arrived(t[5], self.block((q + 2) % 4, 1))


def gather_kernel(rows, feat_own, cot_own, parts, feat, cot, local_sem, send_sem, recv_sem):
    w = Wires(send_sem, recv_sem)
    x, y, z = w.x, w.y, w.z
    me = w.chip * 2 + w.core
    over, beside = (1 - w.chip) * 2 + w.core, w.chip * 2 + 1 - w.core
    across = (1 - w.chip) * 2 + 1 - w.core
    to_over, to_beside = w.at(chip=1 - w.chip), w.at(core=1 - w.core)
    to_across = w.at(chip=1 - w.chip, core=1 - w.core)
    t_z, t_over, t_beside, t_across = (w.ticket() for _ in range(4))
    c_over, c_beside, c_across = (w.ticket() for _ in range(3))
    first_a = RingGather(w, "x", lambda q, h: parts.at[h, q, y, :CUT])
    first_b = RingGather(w, "y", lambda q, h: parts.at[h, x, q, CUT:])
    last_a = RingGather(w, "y", lambda q, h: parts.at[h, :, q, :CUT])
    last_b = RingGather(w, "x", lambda q, h: parts.at[h, q, :, CUT:])

    w.meet(w.everyone())
    w.send(t_z, rows, parts.at[z, x, y], w.at(z=1 - z))
    w.send(t_over, feat_own, feat.at[me], to_over)
    w.send(c_over, cot_own.at[over], cot.at[me], to_over)
    w.send(c_across, cot_own.at[across], cot.at[me], to_across)
    w.send(t_beside, feat_own, feat.at[me], to_beside)
    w.send(c_beside, cot_own.at[beside], cot.at[me], to_beside)
    keep = [
        pltpu.make_async_copy(rows, parts.at[z, x, y], local_sem.at[0]),
        pltpu.make_async_copy(feat_own, feat.at[me], local_sem.at[1]),
        pltpu.make_async_copy(cot_own.at[me], cot.at[me], local_sem.at[2]),
    ]
    for copy in keep:
        copy.start()
    keep[0].wait()
    w.arrived(t_z, parts.at[1 - z, x, y])
    first_a.start()
    first_b.start()
    first_a.forward()
    first_b.forward()
    first_a.end()
    first_b.end()
    last_a.start()
    last_b.start()
    last_a.forward()
    last_b.forward()
    w.arrived(t_over, feat.at[over])
    w.send(t_across, feat.at[over], feat.at[over], to_beside)
    last_a.end()
    last_b.end()
    w.arrived(t_beside, feat.at[beside])
    w.arrived(t_across, feat.at[across])
    w.arrived(c_over, cot.at[over])
    w.arrived(c_beside, cot.at[beside])
    w.arrived(c_across, cot.at[across])
    keep[1].wait()
    keep[2].wait()
    w.finish()


def gather_call(rows, feat_own, cot_own):
    spatial = cot_own.shape[0]
    copies = 7 + 4 * 6
    return pl.pallas_call(
        gather_kernel,
        out_shape=(
            jax.ShapeDtypeStruct((2, 4, 4) + rows.shape, rows.dtype),
            jax.ShapeDtypeStruct((spatial,) + feat_own.shape, feat_own.dtype),
            jax.ShapeDtypeStruct(cot_own.shape, cot_own.dtype),
        ),
        in_specs=[VMEM_SPEC] * 3,
        out_specs=(VMEM_SPEC,) * 3,
        scratch_shapes=[
            pltpu.SemaphoreType.DMA((3,)),
            pltpu.SemaphoreType.DMA((copies,)),
            pltpu.SemaphoreType.DMA((copies,)),
        ],
        compiler_params=pltpu.CompilerParams(
            collective_id=0, has_side_effects=True, vmem_limit_bytes=VMEM_BYTES
        ),
    )(rows, feat_own, cot_own)


class RingReduce:
    def __init__(self, wires, axis, block, near, far_left, far_right):
        self.wires, self.axis, self.block = wires, axis, block
        self.near, self.far = near, (far_left, far_right)
        self.q = getattr(wires, axis)
        self.tickets = [wires.ticket() for _ in range(6)]

    def start(self):
        w, t, q = self.wires, self.tickets, self.q
        right, left = w.step(self.axis, 1), w.step(self.axis, 3)
        w.send(t[0], self.block((q + 2) % 4, 0), self.near.at[0], right)
        w.send(t[1], self.block((q + 2) % 4, 1), self.near.at[1], left)
        w.send(t[2], self.block((q + 1) % 4, 1), self.far[0].at[1], right)
        w.send(t[3], self.block((q + 3) % 4, 0), self.far[1].at[0], left)

    def forward(self):
        w, t, q = self.wires, self.tickets, self.q
        right, left = w.step(self.axis, 1), w.step(self.axis, 3)
        for half, target, other in ((0, (q + 1) % 4, right), (1, (q + 3) % 4, left)):
            w.arrived(t[half], self.near.at[half])
            own = self.block(target, half)[...].astype(jnp.float32)
            self.near[half] = (self.near[half].astype(jnp.float32) + own).astype(jnp.bfloat16)
            w.send(t[4 + half], self.near.at[half], self.far[half].at[half], other)

    def end(self, out):
        w, t, q = self.wires, self.tickets, self.q
        w.arrived(t[2], self.far[0].at[1])
        w.arrived(t[3], self.far[1].at[0])
        w.arrived(t[4], self.far[0].at[0])
        w.arrived(t[5], self.far[1].at[1])
        for half in range(2):
            total = self.block(q, half)[...].astype(jnp.float32)
            total = total + self.far[0][half].astype(jnp.float32)
            total = total + self.far[1][half].astype(jnp.float32)
            out[half] = total.astype(out.dtype)


def reduce_kernel(
    sums, back, grad, total, a_near, a_left, a_right, b_near, b_left, b_right, a_mid, b_mid,
    c_near, c_left, c_right, d_near, d_left, d_right, last, from_z, from_core, to_chip, from_chip,
    send_sem, recv_sem,
):
    w = Wires(send_sem, recv_sem)
    x, y, z, chip, core = w.x, w.y, w.z, w.chip, w.core
    me, over, beside = chip * 2 + core, (1 - chip) * 2 + core, chip * 2 + 1 - core
    across = (1 - chip) * 2 + 1 - core
    to_over, to_beside = w.at(chip=1 - chip), w.at(core=1 - core)
    first_a = RingReduce(w, "y", lambda q, h: sums.at[h, :, q, :CUT], a_near, a_left, a_right)
    first_b = RingReduce(w, "x", lambda q, h: sums.at[h, q, :, CUT:], b_near, b_left, b_right)
    last_a = RingReduce(w, "x", lambda q, h: a_mid.at[h, q], c_near, c_left, c_right)
    last_b = RingReduce(w, "y", lambda q, h: b_mid.at[h, q], d_near, d_left, d_right)
    t_z, t_far, t_own, t_chip = (w.ticket() for _ in range(4))

    w.meet(w.everyone())
    first_a.start()
    first_b.start()
    w.send(t_far, back.at[across], from_core.at[1 - chip], to_beside)
    w.send(t_own, back.at[beside], from_core.at[chip], to_beside)
    w.arrived(t_far, from_core.at[1 - chip])
    to_chip[...] = (
        back[over].astype(jnp.float32) + from_core[1 - chip].astype(jnp.float32)
    ).astype(jnp.bfloat16)
    w.send(t_chip, to_chip, from_chip, to_over)
    first_a.forward()
    first_b.forward()
    w.arrived(t_own, from_core.at[chip])
    total[...] = back[me].astype(jnp.float32) + from_core[chip].astype(jnp.float32)
    first_a.end(a_mid)
    first_b.end(b_mid)
    last_a.start()
    last_b.start()
    last_a.forward()
    last_b.forward()
    last_a.end(last.at[:, :CUT])
    last_b.end(last.at[:, CUT:])
    w.send(t_z, last.at[1 - z], from_z, w.at(z=1 - z))
    w.arrived(t_chip, from_chip)
    total[...] = total[...] + from_chip[...].astype(jnp.float32)
    w.arrived(t_z, from_z)
    grad[...] = last[z].astype(jnp.float32) + from_z[...].astype(jnp.float32)
    w.finish()


def reduce_call(sums, back):
    spatial, capacity, voxels, channels = back.shape
    rest = CHUNK - CUT
    copies = 4 * 6 + 4

    def buffer(*shape):
        return pltpu.VMEM(shape + (LANES,), jnp.bfloat16)

    def ring(*shape):
        return [buffer(2, *shape)] * 3

    block = (capacity, voxels, channels)
    return pl.pallas_call(
        reduce_kernel,
        out_shape=(
            jax.ShapeDtypeStruct((CHUNK, LANES), jnp.float32),
            jax.ShapeDtypeStruct(block, jnp.float32),
        ),
        in_specs=[VMEM_SPEC] * 2,
        out_specs=(VMEM_SPEC,) * 2,
        scratch_shapes=ring(4, CUT)
        + ring(4, rest)
        + [buffer(2, 4, CUT), buffer(2, 4, rest)]
        + ring(CUT)
        + ring(rest)
        + [
            buffer(2, CHUNK),
            buffer(CHUNK),
            pltpu.VMEM((2,) + block, jnp.bfloat16),
            pltpu.VMEM(block, jnp.bfloat16),
            pltpu.VMEM(block, jnp.bfloat16),
            pltpu.SemaphoreType.DMA((copies,)),
            pltpu.SemaphoreType.DMA((copies,)),
        ],
        compiler_params=pltpu.CompilerParams(
            collective_id=1, has_side_effects=True, vmem_limit_bytes=VMEM_BYTES
        ),
    )(sums, back)


def backward_call(table, slots, delta, weight, capacity):
    live, channels = slots.shape[0], weight.shape[0] // 27
    flops = 2 * live * 512 * 27 * channels * LANES
    return pl.pallas_call(
        backward_kernel,
        out_shape=jax.ShapeDtypeStruct((capacity, 512, channels), jnp.bfloat16),
        in_specs=[SMEM_SPEC] * 2 + [VMEM_SPEC] * 2,
        out_specs=VMEM_SPEC,
        scratch_shapes=[
            pltpu.VMEM((live + 1, 64, 8, LANES), jnp.float32),
            pltpu.VMEM((9, live, 10, 64, LANES), jnp.bfloat16),
        ],
        compiler_params=pltpu.CompilerParams(vmem_limit_bytes=VMEM_BYTES),
        cost_estimate=pl.CostEstimate(flops=flops, bytes_accessed=10**7, transcendentals=0),
    )(table, slots, delta, weight)


def live_tables(links):
    group = links.shape[0]
    alive = links[:, 13] >= 0
    order = jnp.arange(group, dtype=jnp.int32)
    before = (order[None, :] < order[:, None]) & alive[None, :]
    rank = jnp.sum(before.astype(jnp.int32), axis=1)
    places = jnp.arange(LIVE, dtype=jnp.int32)
    chosen = ((rank[None, :] == places[:, None]) & alive[None, :]).astype(jnp.int32)
    slots = jnp.sum(chosen * jnp.arange(group, dtype=jnp.int32)[None, :], axis=1)
    rows = jnp.sum(chosen[:, :, None] * links[None, :, :], axis=1)
    named = (rows[:, :, None] == jnp.arange(group, dtype=jnp.int32)).astype(jnp.int32)
    table = jnp.sum(named * (rank - LIVE)[None, None, :], axis=2) + LIVE
    return table.astype(jnp.int32), slots.astype(jnp.int32)


def body(features, cotangent, weight, occupancy, neighbours, first_moment, second_moment):
    channels = features.shape[3]
    capacity = features.shape[1]
    spatial = lax.axis_size("space")
    position = lax.axis_index("space")
    width = channels // spatial
    pad = ((0, 0), (0, 0), (0, LANES - width))
    table, slots = live_tables(neighbours[0])
    own = lax.dynamic_slice_in_dim(occupancy[0], position * capacity, capacity, 0)
    mask = own.astype(jnp.bfloat16)[:, :, None]

    narrow = lax.dynamic_slice_in_dim(weight, position * width, width, 1)
    narrow = jnp.pad(narrow, ((0, CHUNK - narrow.shape[0]), (0, LANES - width)))
    cot = (cotangent[0] * mask).reshape(capacity, 512, spatial, width)
    cot = jnp.pad(cot.transpose(2, 0, 1, 3), ((0, 0),) + pad)
    parts, feat, cot = gather_call(narrow, features[0] * mask, cot)
    feat = feat.reshape(spatial * capacity, 512, channels)
    cot = cot.reshape(spatial * capacity, 512, LANES)

    sums, delta, kernel = forward_call(table, slots, feat, cot, parts)
    back = backward_call(table, slots, delta, kernel, spatial * capacity)
    summed, back = reduce_call(sums, back.reshape(spatial, capacity, 512, channels))
    summed = summed[: weight.shape[0], :width]
    back = back * own.astype(jnp.float32)[:, :, None]
    input_grad = (cotangent[0].astype(jnp.float32) + back).astype(jnp.bfloat16)[None]

    scaled = summed / 64.0
    new_first = 0.9 * first_moment + 0.1 * scaled
    new_second = 0.999 * second_moment + 0.001 * scaled * scaled
    return input_grad, new_first, new_second


def solution(mesh):
    return jax.shard_map(
        body,
        mesh=mesh,
        in_specs=(
            P("dp", "space", None, None),
            P("dp", "space", None, None),
            P("dp", None),
            P("dp", None, None),
            P("dp", None, None),
            P("dp", "space"),
            P("dp", "space"),
        ),
        out_specs=(P("dp", "space", None, None), P("dp", "space"), P("dp", "space")),
        check_vma=False,
    )
```

```python
import jax
import jax.numpy as jnp
from jax import lax
from jax.experimental import pallas as pl
from jax.experimental.pallas import tpu as pltpu
from jax.sharding import PartitionSpec as P

LIVE = 4
LANES = 128
CHUNK = 336
CUT = 176
MESH = pl.DeviceIdType.MESH
VMEM_BYTES = 62 * 1024 * 1024


def fill_regions(table, blocks, regions, live):
    channels = blocks.shape[-1]
    row = lax.broadcasted_iota(jnp.int32, (1, 8, channels), 1)

    def plane(step, carry):
        r = step // 10
        i = step % 10
        first = jnp.where(i == 0, 0, jnp.where(i == 9, 2, 1))
        source = (i + 7) % 8
        code = 9 * first
        for c in range(3):
            pieces = []
            for second, start, count in ((0, 7, 1), (1, 0, 8), (2, 0, 1)):
                where = pl.ds(source * 8 + start, count)
                values = blocks[table[r, code + 3 * second + 1], where]
                if c != 1:
                    edge = blocks[table[r, code + 3 * second + c], where]
                    values = jnp.where(row == (7 if c == 0 else 0), edge, values)
                    values = pltpu.roll(values, 1 if c == 0 else 7, 1)
                pieces.append(values)
            line = jnp.concatenate(pieces, axis=0)
            for b in range(3):
                regions[3 * b + c, r, i] = (
                    line[b : b + 8].reshape(64, channels).astype(jnp.bfloat16)
                )
        return carry

    lax.fori_loop(0, live * 10, plane, 0)


def shifted_rows(regions, block, k, channels):
    a, bc = k // 9, k % 9
    return regions[bc, block, a : a + 8].reshape(512, channels)


SMEM_SPEC = pl.BlockSpec(memory_space=pltpu.SMEM)
VMEM_SPEC = pl.BlockSpec(memory_space=pltpu.VMEM)


class Wires:
    def __init__(self, send_sem, recv_sem):
        self.send_sem, self.recv_sem = send_sem, recv_sem
        dp, space = lax.axis_index("dp"), lax.axis_index("space")
        self.x, self.y, self.z = dp // 8, dp // 2 % 4, dp % 2
        self.chip, self.core = space // 2, space % 2
        self.started = []
        self.count = 0

    def at(self, x=None, y=None, z=None, chip=None, core=None):
        x, y, z = self.x if x is None else x, self.y if y is None else y, self.z if z is None else z
        chip, core = self.chip if chip is None else chip, self.core if core is None else core
        return (x * 8 + y * 2 + z, chip * 2 + core)

    def step(self, axis, by):
        return self.at(**{axis: (getattr(self, axis) + by) % 4})

    def meet(self, others):
        barrier = pltpu.get_barrier_semaphore()
        for other in others:
            pl.semaphore_signal(barrier, inc=1, device_id=other, device_id_type=MESH)
        pl.semaphore_wait(barrier, len(others))

    def everyone(self):
        return (
            [self.step(axis, by) for axis in ("x", "y") for by in (1, 3)]
            + [self.at(z=1 - self.z), self.at(chip=1 - self.chip), self.at(core=1 - self.core)]
            + [self.at(chip=1 - self.chip, core=1 - self.core)]
        )

    def ticket(self):
        self.count += 1
        return self.count - 1

    def send(self, ticket, source, target, other):
        copy = pltpu.make_async_remote_copy(
            source,
            target,
            self.send_sem.at[ticket],
            self.recv_sem.at[ticket],
            device_id=other,
            device_id_type=MESH,
        )
        copy.start()
        self.started.append(copy)

    def arrived(self, ticket, landing):
        pltpu.make_async_remote_copy(
            landing,
            landing,
            self.send_sem.at[ticket],
            self.recv_sem.at[ticket],
            device_id=self.at(core=1 - self.core),
            device_id_type=MESH,
        ).wait_recv()

    def finish(self):
        for copy in self.started:
            copy.wait_send()
        self.started = []


class RingGather:
    def __init__(self, wires, axis, block):
        self.wires, self.axis, self.block = wires, axis, block
        self.q = getattr(wires, axis)
        self.tickets = [wires.ticket() for _ in range(6)]

    def start(self):
        t, q = self.tickets, self.q
        right, left = self.wires.step(self.axis, 1), self.wires.step(self.axis, 3)
        for ticket, half, other in ((t[0], 0, right), (t[1], 1, left), (t[2], 1, right), (t[3], 0, left)):
            mine = self.block(q, half)
            self.wires.send(ticket, mine, mine, other)

    def forward(self):
        t, q = self.tickets, self.q
        right, left = self.wires.step(self.axis, 1), self.wires.step(self.axis, 3)
        for ticket, into, half, source, other in (
            (t[0], t[4], 0, (q + 3) % 4, right),
            (t[1], t[5], 1, (q + 1) % 4, left),
        ):
            piece = self.block(source, half)
            self.wires.arrived(ticket, piece)
            self.wires.send(into, piece, piece, other)

    def end(self):
        t, q = self.tickets, self.q
        self.wires.arrived(t[2], self.block((q + 3) % 4, 1))
        self.wires.arrived(t[3], self.block((q + 1) % 4, 0))
        self.wires.arrived(t[4], self.block((q + 2) % 4, 0))
        self.wires.arrived(t[5], self.block((q + 2) % 4, 1))


class RingReduce:
    def __init__(self, wires, axis, block, near, far_left, far_right):
        self.wires, self.axis, self.block = wires, axis, block
        self.near, self.far = near, (far_left, far_right)
        self.q = getattr(wires, axis)
        self.tickets = [wires.ticket() for _ in range(6)]

    def start(self):
        w, t, q = self.wires, self.tickets, self.q
        right, left = w.step(self.axis, 1), w.step(self.axis, 3)
        w.send(t[0], self.block((q + 2) % 4, 0), self.near.at[0], right)
        w.send(t[1], self.block((q + 2) % 4, 1), self.near.at[1], left)
        w.send(t[2], self.block((q + 1) % 4, 1), self.far[0].at[1], right)
        w.send(t[3], self.block((q + 3) % 4, 0), self.far[1].at[0], left)

    def forward(self):
        w, t, q = self.wires, self.tickets, self.q
        right, left = w.step(self.axis, 1), w.step(self.axis, 3)
        for half, target, other in ((0, (q + 1) % 4, right), (1, (q + 3) % 4, left)):
            w.arrived(t[half], self.near.at[half])
            own = self.block(target, half)[...].astype(jnp.float32)
            self.near[half] = (self.near[half].astype(jnp.float32) + own).astype(jnp.bfloat16)
            w.send(t[4 + half], self.near.at[half], self.far[half].at[half], other)

    def end(self, out):
        w, t, q = self.wires, self.tickets, self.q
        w.arrived(t[2], self.far[0].at[1])
        w.arrived(t[3], self.far[1].at[0])
        w.arrived(t[4], self.far[0].at[0])
        w.arrived(t[5], self.far[1].at[1])
        for half in range(2):
            total = self.block(q, half)[...].astype(jnp.float32)
            total = total + self.far[0][half].astype(jnp.float32)
            total = total + self.far[1][half].astype(jnp.float32)
            out[half] = total.astype(out.dtype)


def step_kernel(
    table, slots, places, rows, feat_own, cot_own, grad, total,
    parts, feat, cot, blocks, regions, delta, delta_t, stage, weight, thin, back_live, back,
    a_near, a_left, a_right, b_near, b_left, b_right, a_mid, b_mid,
    c_near, c_left, c_right, d_near, d_left, d_right, last, from_z, from_core, to_chip, from_chip,
    local_sem, send_sem, recv_sem,
):
    live, group = slots.shape[0], places.shape[0]
    capacity, channels = feat_own.shape[0], feat_own.shape[2]
    rows_of = 27 * channels // 32
    w = Wires(send_sem, recv_sem)
    x, y, z, chip, core = w.x, w.y, w.z, w.chip, w.core
    me, over, beside = chip * 2 + core, (1 - chip) * 2 + core, chip * 2 + 1 - core
    across = (1 - chip) * 2 + 1 - core
    to_over, to_beside = w.at(chip=1 - chip), w.at(core=1 - core)
    to_across = w.at(chip=1 - chip, core=1 - core)
    t_z, t_over, t_beside, t_across = (w.ticket() for _ in range(4))
    c_over, c_beside, c_across = (w.ticket() for _ in range(3))
    first_a = RingGather(w, "x", lambda q, h: parts.at[h, q, y, :CUT])
    first_b = RingGather(w, "y", lambda q, h: parts.at[h, x, q, CUT:])
    last_a = RingGather(w, "y", lambda q, h: parts.at[h, :, q, :CUT])
    last_b = RingGather(w, "x", lambda q, h: parts.at[h, q, :, CUT:])
    sum_a = RingReduce(w, "y", lambda q, h: parts.at[h, :, q, :CUT], a_near, a_left, a_right)
    sum_b = RingReduce(w, "x", lambda q, h: parts.at[h, q, :, CUT:], b_near, b_left, b_right)
    end_a = RingReduce(w, "x", lambda q, h: a_mid.at[h, q], c_near, c_left, c_right)
    end_b = RingReduce(w, "y", lambda q, h: b_mid.at[h, q], d_near, d_left, d_right)
    t_out, t_far, t_own, t_chip = (w.ticket() for _ in range(4))

    w.meet(w.everyone())
    w.send(t_z, rows, parts.at[z, x, y], w.at(z=1 - z))
    w.send(t_over, feat_own, feat.at[me], to_over)
    w.send(t_beside, feat_own, feat.at[me], to_beside)
    w.send(c_beside, cot_own.at[beside], cot.at[me], to_beside)
    keep = [
        pltpu.make_async_copy(rows, parts.at[z, x, y], local_sem.at[0]),
        pltpu.make_async_copy(feat_own, feat.at[me], local_sem.at[1]),
        pltpu.make_async_copy(cot_own.at[me], cot.at[me], local_sem.at[2]),
    ]
    for copy in keep:
        copy.start()
    keep[0].wait()
    w.arrived(t_z, parts.at[1 - z, x, y])
    first_a.start()
    first_b.start()
    first_a.forward()
    first_b.forward()
    first_a.end()
    first_b.end()
    last_a.start()
    last_b.start()
    w.arrived(t_over, feat.at[over])
    w.send(t_across, feat.at[over], feat.at[over], to_beside)
    w.send(c_over, cot_own.at[over], cot.at[me], to_over)
    w.send(c_across, cot_own.at[across], cot.at[me], to_across)
    last_a.forward()
    last_b.forward()
    keep[1].wait()
    keep[2].wait()
    w.arrived(t_beside, feat.at[beside])
    w.arrived(t_across, feat.at[across])

    for r in range(live):
        blocks[r] = feat[slots[r] // capacity, slots[r] % capacity].astype(jnp.float32).reshape(
            64, 8, channels
        )
    blocks[live] = jnp.zeros((64, 8, channels), jnp.float32)
    fill_regions(table, blocks, regions, live)
    last_a.end()
    last_b.end()
    for d in range(32):
        stage[rows_of * d : rows_of * d + CHUNK] = parts[d % 2, d // 8, d // 2 % 4].astype(
            jnp.float32
        )
    for k in range(27):
        weight[k * channels : (k + 1) * channels] = stage[
            pl.ds(k, channels, stride=27), :
        ].astype(jnp.bfloat16)
    w.arrived(c_over, cot.at[over])
    w.arrived(c_beside, cot.at[beside])
    w.arrived(c_across, cot.at[across])

    def forward_block(r, carry):
        pre = jnp.zeros((512, LANES), jnp.float32)
        for ks in (range(g, min(g + 2, 27)) for g in range(0, 27, 2)):
            lhs = jnp.concatenate([shifted_rows(regions, r, k, channels) for k in ks], axis=1)
            rhs = weight[ks[0] * channels : (ks[-1] + 1) * channels]
            pre = pre + jnp.dot(lhs, rhs, preferred_element_type=jnp.float32)
        gate = jax.nn.sigmoid(pre)
        value = cot[slots[r] // capacity, slots[r] % capacity].astype(jnp.float32)
        delta[r] = (value * gate * (1.0 + pre * (1.0 - gate))).astype(jnp.bfloat16)
        return carry

    lax.fori_loop(0, live, forward_block, 0)
    for r in range(live):
        delta_t[:, r * 512 : (r + 1) * 512] = (
            delta[r].astype(jnp.float32).T.astype(jnp.bfloat16)
        )
    for k in range(27):
        field = jnp.concatenate(
            [shifted_rows(regions, r, k, channels) for r in range(live)], axis=0
        )
        part = jnp.dot(delta_t[...], field, preferred_element_type=jnp.float32)
        stage[pl.ds(k, channels, stride=27), :] = part.T
    w.finish()
    for d in range(32):
        parts[d % 2, d // 8, d // 2 % 4] = stage[rows_of * d : rows_of * d + CHUNK].astype(
            jnp.bfloat16
        )
    sum_a.start()
    sum_b.start()

    for r in range(live):
        thin[r] = delta[r].astype(jnp.float32).reshape(64, 8, LANES)
    thin[live] = jnp.zeros((64, 8, LANES), jnp.float32)
    narrow = regions.at[:, :, :, :, :LANES]
    fill_regions(table, thin, narrow, live)
    back_live[live] = jnp.zeros((512, channels), jnp.bfloat16)

    def back_block(r, carry):
        out = jnp.zeros((512, channels), jnp.float32)
        for ks in (range(g, min(g + 4, 27)) for g in range(0, 27, 4)):
            lhs = jnp.concatenate([shifted_rows(narrow, r, 26 - k, LANES) for k in ks], axis=1)
            rhs = jnp.concatenate(
                [weight[k * channels : (k + 1) * channels] for k in ks], axis=1
            )
            out = out + lax.dot_general(
                lhs, rhs, (((1,), (1,)), ((), ())), preferred_element_type=jnp.float32
            )
        back_live[r] = out.astype(jnp.bfloat16)
        return carry

    lax.fori_loop(0, live // 2, back_block, 0)
    sum_a.forward()
    sum_b.forward()
    lax.fori_loop(live // 2, live, back_block, 0)
    for slot in range(group):
        back[slot // capacity, slot % capacity] = back_live[places[slot]]
    w.send(t_far, back.at[across], from_core.at[1 - chip], to_beside)
    w.send(t_own, back.at[beside], from_core.at[chip], to_beside)
    sum_a.end(a_mid)
    sum_b.end(b_mid)
    end_a.start()
    end_b.start()
    w.arrived(t_far, from_core.at[1 - chip])
    to_chip[...] = (
        back[over].astype(jnp.float32) + from_core[1 - chip].astype(jnp.float32)
    ).astype(jnp.bfloat16)
    w.send(t_chip, to_chip, from_chip, to_over)
    end_a.forward()
    end_b.forward()
    w.arrived(t_own, from_core.at[chip])
    total[...] = back[me].astype(jnp.float32) + from_core[chip].astype(jnp.float32)
    end_a.end(last.at[:, :CUT])
    end_b.end(last.at[:, CUT:])
    w.send(t_out, last.at[1 - z], from_z, w.at(z=1 - z))
    w.arrived(t_out, from_z)
    grad[...] = last[z].astype(jnp.float32) + from_z[...].astype(jnp.float32)
    w.arrived(t_chip, from_chip)
    total[...] = total[...] + from_chip[...].astype(jnp.float32)
    w.finish()


def step_call(table, slots, places, rows, feat_own, cot_own):
    live, spatial = slots.shape[0], cot_own.shape[0]
    channels = feat_own.shape[2]
    rest = CHUNK - CUT
    copies = 8 * 6 + 11

    def buffer(*shape):
        return pltpu.VMEM(shape, jnp.bfloat16)

    def wide(*shape):
        return pltpu.VMEM(shape, jnp.float32)

    def ring(*shape):
        return [buffer(2, *shape, LANES)] * 3

    block = feat_own.shape
    flops = 3 * 2 * live * 512 * 27 * channels * LANES
    return pl.pallas_call(
        step_kernel,
        out_shape=(
            jax.ShapeDtypeStruct((CHUNK, LANES), jnp.float32),
            jax.ShapeDtypeStruct(block, jnp.float32),
        ),
        in_specs=[SMEM_SPEC] * 3 + [VMEM_SPEC] * 3,
        out_specs=(VMEM_SPEC,) * 2,
        scratch_shapes=[
            buffer(2, 4, 4, CHUNK, LANES),
            buffer(spatial, *block),
            buffer(*cot_own.shape),
            wide(live + 1, 64, 8, channels),
            buffer(9, live, 10, 64, channels),
            buffer(live, 512, LANES),
            buffer(LANES, live * 512),
            wide(27 * channels + 16, LANES),
            buffer(27 * channels, LANES),
            wide(live + 1, 64, 8, LANES),
            buffer(live + 1, 512, channels),
            buffer(spatial, *block),
        ]
        + ring(4, CUT)
        + ring(4, rest)
        + [buffer(2, 4, CUT, LANES), buffer(2, 4, rest, LANES)]
        + ring(CUT)
        + ring(rest)
        + [
            buffer(2, CHUNK, LANES),
            buffer(CHUNK, LANES),
            buffer(2, *block),
            buffer(*block),
            buffer(*block),
            pltpu.SemaphoreType.DMA((3,)),
            pltpu.SemaphoreType.DMA((copies,)),
            pltpu.SemaphoreType.DMA((copies,)),
        ],
        compiler_params=pltpu.CompilerParams(
            collective_id=0, has_side_effects=True, vmem_limit_bytes=VMEM_BYTES
        ),
        cost_estimate=pl.CostEstimate(flops=flops, bytes_accessed=10**7, transcendentals=10**6),
    )(table, slots, places, rows, feat_own, cot_own)


def live_tables(links):
    group = links.shape[0]
    alive = links[:, 13] >= 0
    order = jnp.arange(group, dtype=jnp.int32)
    before = (order[None, :] < order[:, None]) & alive[None, :]
    rank = jnp.sum(before.astype(jnp.int32), axis=1)
    places = jnp.arange(LIVE, dtype=jnp.int32)
    chosen = ((rank[None, :] == places[:, None]) & alive[None, :]).astype(jnp.int32)
    slots = jnp.sum(chosen * jnp.arange(group, dtype=jnp.int32)[None, :], axis=1)
    rows = jnp.sum(chosen[:, :, None] * links[None, :, :], axis=1)
    named = (rows[:, :, None] == jnp.arange(group, dtype=jnp.int32)).astype(jnp.int32)
    table = jnp.sum(named * (rank - LIVE)[None, None, :], axis=2) + LIVE
    places = jnp.where(alive, rank, LIVE)
    return table.astype(jnp.int32), slots.astype(jnp.int32), places.astype(jnp.int32)


def body(features, cotangent, weight, occupancy, neighbours, first_moment, second_moment):
    channels = features.shape[3]
    capacity = features.shape[1]
    spatial = lax.axis_size("space")
    position = lax.axis_index("space")
    width = channels // spatial
    pad = ((0, 0), (0, 0), (0, LANES - width))
    table, slots, places = live_tables(neighbours[0])
    own = lax.dynamic_slice_in_dim(occupancy[0], position * capacity, capacity, 0)
    mask = own.astype(jnp.bfloat16)[:, :, None]

    narrow = lax.dynamic_slice_in_dim(weight, position * width, width, 1)
    narrow = jnp.pad(narrow, ((0, CHUNK - narrow.shape[0]), (0, LANES - width)))
    cot = (cotangent[0] * mask).reshape(capacity, 512, spatial, width)
    cot = jnp.pad(cot.transpose(2, 0, 1, 3), ((0, 0),) + pad)
    summed, back = step_call(table, slots, places, narrow, features[0] * mask, cot)
    summed = summed[: weight.shape[0], :width]
    back = back * own.astype(jnp.float32)[:, :, None]
    input_grad = (cotangent[0].astype(jnp.float32) + back).astype(jnp.bfloat16)[None]

    scaled = summed / 64.0
    new_first = 0.9 * first_moment + 0.1 * scaled
    new_second = 0.999 * second_moment + 0.001 * scaled * scaled
    return input_grad, new_first, new_second


def solution(mesh):
    return jax.shard_map(
        body,
        mesh=mesh,
        in_specs=(
            P("dp", "space", None, None),
            P("dp", "space", None, None),
            P("dp", None),
            P("dp", None, None),
            P("dp", None, None),
            P("dp", "space"),
            P("dp", "space"),
        ),
        out_specs=(P("dp", "space", None, None), P("dp", "space"), P("dp", "space")),
        check_vma=False,
    )
```

```python
import jax
import jax.numpy as jnp
from jax import lax
from jax.experimental import pallas as pl
from jax.experimental.pallas import tpu as pltpu
from jax.sharding import PartitionSpec as P

LIVE = 4
LANES = 128
CHUNK = 336
CUT = 176
MESH = pl.DeviceIdType.MESH
VMEM_BYTES = 62 * 1024 * 1024


def fill_regions(table, blocks, regions, live):
    channels = blocks.shape[-1]
    row = lax.broadcasted_iota(jnp.int32, (1, 8, channels), 1)

    def plane(step, carry):
        r = step // 10
        i = step % 10
        first = jnp.where(i == 0, 0, jnp.where(i == 9, 2, 1))
        source = (i + 7) % 8
        code = 9 * first
        for c in range(3):
            pieces = []
            for second, start, count in ((0, 7, 1), (1, 0, 8), (2, 0, 1)):
                where = pl.ds(source * 8 + start, count)
                values = blocks[table[r, code + 3 * second + 1], where]
                if c != 1:
                    edge = blocks[table[r, code + 3 * second + c], where]
                    values = jnp.where(row == (7 if c == 0 else 0), edge, values)
                    values = pltpu.roll(values, 1 if c == 0 else 7, 1)
                pieces.append(values)
            line = jnp.concatenate(pieces, axis=0)
            for b in range(3):
                regions[3 * b + c, r, i] = (
                    line[b : b + 8].reshape(64, channels).astype(jnp.bfloat16)
                )
        return carry

    lax.fori_loop(0, live * 10, plane, 0)


def shifted_rows(regions, block, k, channels):
    a, bc = k // 9, k % 9
    return regions[bc, block, a : a + 8].reshape(512, channels)


SMEM_SPEC = pl.BlockSpec(memory_space=pltpu.SMEM)
VMEM_SPEC = pl.BlockSpec(memory_space=pltpu.VMEM)


class Wires:
    def __init__(self, send_sem, recv_sem):
        self.send_sem, self.recv_sem = send_sem, recv_sem
        dp, space = lax.axis_index("dp"), lax.axis_index("space")
        self.x, self.y, self.z = dp // 8, dp // 2 % 4, dp % 2
        self.chip, self.core = space // 2, space % 2
        self.started = []
        self.count = 0

    def at(self, x=None, y=None, z=None, chip=None, core=None):
        x, y, z = self.x if x is None else x, self.y if y is None else y, self.z if z is None else z
        chip, core = self.chip if chip is None else chip, self.core if core is None else core
        return (x * 8 + y * 2 + z, chip * 2 + core)

    def step(self, axis, by):
        return self.at(**{axis: (getattr(self, axis) + by) % 4})

    def greet(self, others):
        barrier = pltpu.get_barrier_semaphore()
        for other in others:
            pl.semaphore_signal(barrier, inc=1, device_id=other, device_id_type=MESH)

    def met(self, others):
        pl.semaphore_wait(pltpu.get_barrier_semaphore(), len(others))

    def everyone(self):
        return (
            [self.step(axis, by) for axis in ("x", "y") for by in (1, 3)]
            + [self.at(z=1 - self.z), self.at(chip=1 - self.chip), self.at(core=1 - self.core)]
            + [self.at(chip=1 - self.chip, core=1 - self.core)]
        )

    def ticket(self):
        self.count += 1
        return self.count - 1

    def send(self, ticket, source, target, other):
        copy = pltpu.make_async_remote_copy(
            source,
            target,
            self.send_sem.at[ticket],
            self.recv_sem.at[ticket],
            device_id=other,
            device_id_type=MESH,
        )
        copy.start()
        self.started.append(copy)

    def arrived(self, ticket, landing):
        pltpu.make_async_remote_copy(
            landing,
            landing,
            self.send_sem.at[ticket],
            self.recv_sem.at[ticket],
            device_id=self.at(core=1 - self.core),
            device_id_type=MESH,
        ).wait_recv()

    def finish(self):
        for copy in self.started:
            copy.wait_send()
        self.started = []


class RingGather:
    def __init__(self, wires, axis, block):
        self.wires, self.axis, self.block = wires, axis, block
        self.q = getattr(wires, axis)
        self.tickets = [wires.ticket() for _ in range(6)]

    def start(self):
        t, q = self.tickets, self.q
        right, left = self.wires.step(self.axis, 1), self.wires.step(self.axis, 3)
        for ticket, half, other in ((t[0], 0, right), (t[1], 1, left), (t[2], 1, right), (t[3], 0, left)):
            mine = self.block(q, half)
            self.wires.send(ticket, mine, mine, other)

    def forward(self):
        t, q = self.tickets, self.q
        right, left = self.wires.step(self.axis, 1), self.wires.step(self.axis, 3)
        for ticket, into, half, source, other in (
            (t[0], t[4], 0, (q + 3) % 4, right),
            (t[1], t[5], 1, (q + 1) % 4, left),
        ):
            piece = self.block(source, half)
            self.wires.arrived(ticket, piece)
            self.wires.send(into, piece, piece, other)

    def end(self):
        t, q = self.tickets, self.q
        self.wires.arrived(t[2], self.block((q + 3) % 4, 1))
        self.wires.arrived(t[3], self.block((q + 1) % 4, 0))
        self.wires.arrived(t[4], self.block((q + 2) % 4, 0))
        self.wires.arrived(t[5], self.block((q + 2) % 4, 1))


class RingReduce:
    def __init__(self, wires, axis, block, near, far_left, far_right):
        self.wires, self.axis, self.block = wires, axis, block
        self.near, self.far = near, (far_left, far_right)
        self.q = getattr(wires, axis)
        self.tickets = [wires.ticket() for _ in range(6)]

    def start(self):
        w, t, q = self.wires, self.tickets, self.q
        right, left = w.step(self.axis, 1), w.step(self.axis, 3)
        w.send(t[0], self.block((q + 2) % 4, 0), self.near.at[0], right)
        w.send(t[1], self.block((q + 2) % 4, 1), self.near.at[1], left)
        w.send(t[2], self.block((q + 1) % 4, 1), self.far[0].at[1], right)
        w.send(t[3], self.block((q + 3) % 4, 0), self.far[1].at[0], left)

    def forward(self):
        w, t, q = self.wires, self.tickets, self.q
        right, left = w.step(self.axis, 1), w.step(self.axis, 3)
        for half, target, other in ((0, (q + 1) % 4, right), (1, (q + 3) % 4, left)):
            w.arrived(t[half], self.near.at[half])
            own = self.block(target, half)[...].astype(jnp.float32)
            self.near[half] = (self.near[half].astype(jnp.float32) + own).astype(jnp.bfloat16)
            w.send(t[4 + half], self.near.at[half], self.far[half].at[half], other)

    def end(self, out):
        w, t, q = self.wires, self.tickets, self.q
        w.arrived(t[2], self.far[0].at[1])
        w.arrived(t[3], self.far[1].at[0])
        w.arrived(t[4], self.far[0].at[0])
        w.arrived(t[5], self.far[1].at[1])
        for half in range(2):
            total = self.block(q, half)[...].astype(jnp.float32)
            total = total + self.far[0][half].astype(jnp.float32)
            total = total + self.far[1][half].astype(jnp.float32)
            out[half] = total.astype(out.dtype)


def read_links(links, chip, table, slots, place, order, inward, onward):
    group = links.shape[1]
    alive = [(links[0, s, 13] >= 0).astype(jnp.int32) for s in range(group)]
    near = [(chip == s // (group // 2)).astype(jnp.int32) for s in range(group)]
    others = sum(a * (1 - n) for a, n in zip(alive, near))
    rank, counts, position = [], [0, 0], []
    total = 0
    for s in range(group):
        side = s // (group // 2)
        rank.append(total)
        position.append(counts[side] + near[s] * others)
        place[s + 1] = jnp.where(alive[s] > 0, jnp.minimum(total, LIVE), LIVE)
        inward[s] = jnp.where(alive[s] > 0, jnp.minimum(counts[side], LIVE), LIVE)
        onward[s] = jnp.where(alive[s] > 0, jnp.minimum(position[s], LIVE), LIVE)
        total = total + alive[s]
        counts[side] = counts[side] + alive[s]
    place[0] = LIVE
    for r in range(LIVE):
        slots[r] = sum(jnp.where(rank[s] == r, alive[s] * s, 0) for s in range(group))
        turn = sum(jnp.where(position[s] == r, alive[s] * rank[s], 0) for s in range(group))
        order[r] = jnp.minimum(turn, LIVE - 1)

    def code_of(code, carry):
        for r in range(LIVE):
            table[r, code] = place[links[0, slots[r], code] + 1]
        return carry

    lax.fori_loop(0, 27, code_of, 0)


def lanes_from(values, start, width):
    turned = pltpu.roll(values, (values.shape[1] - start) % values.shape[1], 1)[:, :LANES]
    lane = lax.broadcasted_iota(jnp.int32, turned.shape, 1)
    return jnp.where(lane < width, turned, 0.0).astype(jnp.bfloat16)


def step_kernel(
    links, occupancy, features, cotangent, shard, input_grad, grad,
    rows, cot_own, mask, table, slots, place, order, inward, onward,
    parts, feat, cot, blocks, regions, delta, delta_t, stage, weight, thin,
    a_near, a_left, a_right, b_near, b_left, b_right, a_mid, b_mid,
    c_near, c_left, c_right, d_near, d_left, d_right, last, from_z,
    halves, inbox, chip_sum, z_out, z_in, fin_out, fin_in,
    local_sem, send_sem, recv_sem,
):
    live, group = LIVE, links.shape[1]
    capacity, voxels, channels = features.shape[1:]
    spatial = group // capacity
    width = channels // spatial
    rows_of = shard.shape[0]
    half = voxels // 2
    w = Wires(send_sem, recv_sem)
    x, y, z, chip, core = w.x, w.y, w.z, w.chip, w.core
    me, over, beside = chip * 2 + core, (1 - chip) * 2 + core, chip * 2 + 1 - core
    across = (1 - chip) * 2 + 1 - core
    to_over, to_beside = w.at(chip=1 - chip), w.at(core=1 - core)
    to_across = w.at(chip=1 - chip, core=1 - core)
    t_z, t_over, t_beside, t_across = (w.ticket() for _ in range(4))
    c_over, c_beside, c_across = (w.ticket() for _ in range(3))
    first_a = RingGather(w, "x", lambda q, h: parts.at[h, q, y, :CUT])
    first_b = RingGather(w, "y", lambda q, h: parts.at[h, x, q, CUT:])
    last_a = RingGather(w, "y", lambda q, h: parts.at[h, :, q, :CUT])
    last_b = RingGather(w, "x", lambda q, h: parts.at[h, q, :, CUT:])
    sum_a = RingReduce(w, "y", lambda q, h: parts.at[h, :, q, :CUT], a_near, a_left, a_right)
    sum_b = RingReduce(w, "x", lambda q, h: parts.at[h, q, :, CUT:], b_near, b_left, b_right)
    end_a = RingReduce(w, "x", lambda q, h: a_mid.at[h, q], c_near, c_left, c_right)
    end_b = RingReduce(w, "y", lambda q, h: b_mid.at[h, q], d_near, d_left, d_right)
    t_out, t_fin = w.ticket(), w.ticket()
    t_core = [w.ticket() for _ in range(live)]
    t_chip = [w.ticket() for _ in range(live)]

    w.greet(w.everyone())
    rows[CHUNK - 16 :] = jnp.zeros((16, LANES), jnp.bfloat16)
    start = (spatial - me) % spatial * width
    turned = pltpu.roll(shard[...].astype(jnp.float32), start, 1)[:, :LANES]
    lane = lax.broadcasted_iota(jnp.int32, turned.shape, 1)
    rows[:rows_of] = jnp.where(lane < width, turned, 0.0).astype(jnp.bfloat16)
    w.met(w.everyone())
    w.send(t_z, rows, parts.at[z, x, y], w.at(z=1 - z))
    w.send(t_over, features.at[0], feat.at[me], to_over)
    w.send(t_beside, features.at[0], feat.at[me], to_beside)
    keep = [
        pltpu.make_async_copy(rows, parts.at[z, x, y], local_sem.at[0]),
        pltpu.make_async_copy(features.at[0], feat.at[me], local_sem.at[1]),
    ]
    for copy in keep:
        copy.start()
    read_links(links, chip, table, slots, place, order, inward, onward)
    keep[0].wait()
    w.arrived(t_z, parts.at[1 - z, x, y])
    first_a.start()
    first_b.start()
    for s in range(spatial):
        for n in range(capacity):
            cot_own[s, n] = lanes_from(cotangent[0, n].astype(jnp.float32), s * width, width)
    cot[me] = cot_own[me]
    w.send(c_beside, cot_own.at[beside], cot.at[me], to_beside)
    held = occupancy[0].astype(jnp.float32)
    held = jnp.concatenate([held] * (LANES // group), axis=0).T
    for s in range(group):
        mask[s] = jnp.broadcast_to(held[:, s : s + 1], (voxels, LANES))
    first_a.forward()
    first_b.forward()
    first_a.end()
    first_b.end()
    last_a.start()
    last_b.start()
    w.arrived(t_over, feat.at[over])
    w.send(t_across, feat.at[over], feat.at[over], to_beside)
    w.send(c_over, cot_own.at[over], cot.at[me], to_over)
    w.send(c_across, cot_own.at[across], cot.at[me], to_across)
    last_a.forward()
    last_b.forward()
    keep[1].wait()
    w.arrived(t_beside, feat.at[beside])
    w.arrived(t_across, feat.at[across])

    for r in range(live):
        full = jnp.concatenate([mask[slots[r]]] * (channels // LANES), axis=1)
        field = feat[slots[r] // capacity, slots[r] % capacity].astype(jnp.float32)
        blocks[r] = (field * full).reshape(64, 8, channels)
    blocks[live] = jnp.zeros((64, 8, channels), jnp.float32)
    fill_regions(table, blocks, regions, live)
    last_a.end()
    last_b.end()
    for d in range(32):
        stage[rows_of * d : rows_of * d + CHUNK] = parts[d % 2, d // 8, d // 2 % 4].astype(
            jnp.float32
        )
    for k in range(27):
        weight[k * channels : (k + 1) * channels] = stage[
            pl.ds(k, channels, stride=27), :
        ].astype(jnp.bfloat16)
    w.arrived(c_over, cot.at[over])
    w.arrived(c_beside, cot.at[beside])
    w.arrived(c_across, cot.at[across])

    def forward_block(r, carry):
        pre = jnp.zeros((512, LANES), jnp.float32)
        for ks in (range(g, min(g + 2, 27)) for g in range(0, 27, 2)):
            lhs = jnp.concatenate([shifted_rows(regions, r, k, channels) for k in ks], axis=1)
            rhs = weight[ks[0] * channels : (ks[-1] + 1) * channels]
            pre = pre + jnp.dot(lhs, rhs, preferred_element_type=jnp.float32)
        gate = jax.nn.sigmoid(pre)
        value = cot[slots[r] // capacity, slots[r] % capacity].astype(jnp.float32)
        delta[r] = (value * mask[slots[r]] * gate * (1.0 + pre * (1.0 - gate))).astype(jnp.bfloat16)
        return carry

    lax.fori_loop(0, live, forward_block, 0)
    for r in range(live):
        delta_t[:, r * 512 : (r + 1) * 512] = (
            delta[r].astype(jnp.float32).T.astype(jnp.bfloat16)
        )
    for k in range(27):
        field = jnp.concatenate(
            [shifted_rows(regions, r, k, channels) for r in range(live)], axis=0
        )
        part = jnp.dot(delta_t[...], field, preferred_element_type=jnp.float32)
        stage[pl.ds(k, channels, stride=27), :] = part.T
    w.finish()
    for d in range(32):
        parts[d % 2, d // 8, d // 2 % 4] = stage[rows_of * d : rows_of * d + CHUNK].astype(
            jnp.bfloat16
        )
    sum_a.start()
    sum_b.start()

    for r in range(live):
        thin[r] = delta[r].astype(jnp.float32).reshape(64, 8, LANES)
    thin[live] = jnp.zeros((64, 8, LANES), jnp.float32)
    narrow = regions.at[:, :, :, :, :LANES]
    fill_regions(table, thin, narrow, live)

    chip_sum[live] = jnp.zeros((half, channels), jnp.float32)
    z_in[live] = jnp.zeros((half, channels), jnp.bfloat16)

    def back_block(j):
        r = order[j]
        out = jnp.zeros((voxels, channels), jnp.float32)
        for ks in (range(g, min(g + 4, 27)) for g in range(0, 27, 4)):
            lhs = jnp.concatenate([shifted_rows(narrow, r, 26 - k, LANES) for k in ks], axis=1)
            rhs = jnp.concatenate(
                [weight[k * channels : (k + 1) * channels] for k in ks], axis=1
            )
            out = out + lax.dot_general(
                lhs, rhs, (((1,), (1,)), ((), ())), preferred_element_type=jnp.float32
            )
        halves[j] = out.astype(jnp.bfloat16).reshape(2, half, channels)
        w.send(t_core[j], halves.at[j, 1 - core], inbox.at[j], to_beside)

    def join(j):
        w.arrived(t_core[j], inbox.at[j])
        value = halves[j, core].astype(jnp.float32) + inbox[j].astype(jnp.float32)
        chip_sum[j] = value
        z_out[j] = value.astype(jnp.bfloat16)
        w.send(t_chip[j], z_out.at[j], z_in.at[j], to_over)

    back_block(0)
    back_block(1)
    join(0)
    sum_a.forward()
    sum_b.forward()
    back_block(2)
    join(1)
    back_block(3)
    join(2)
    sum_a.end(a_mid)
    sum_b.end(b_mid)
    end_a.start()
    end_b.start()
    join(3)
    end_a.forward()
    end_b.forward()
    end_a.end(last.at[:, :CUT])
    end_b.end(last.at[:, CUT:])
    w.send(t_out, last.at[1 - z], from_z, w.at(z=1 - z))
    for j in range(live):
        w.arrived(t_chip[j], z_in.at[j])

    def whole(owner, n):
        s = owner * capacity + n
        return z_in[inward[s]].astype(jnp.float32) + chip_sum[onward[s]]

    def finish(n, part, value):
        span = pl.ds(pl.multiple_of(part * half, half), half)
        full = jnp.concatenate([mask[me * capacity + n, span]] * (channels // LANES), axis=1)
        value = cotangent[0, n, span].astype(jnp.float32) + full * value
        input_grad[0, n, span] = value.astype(jnp.bfloat16)

    for n in range(capacity):
        fin_out[n] = whole(beside, n).astype(jnp.bfloat16)
    w.send(t_fin, fin_out, fin_in, to_beside)
    for n in range(capacity):
        finish(n, core, whole(me, n))
    w.arrived(t_out, from_z)
    done = last[z].astype(jnp.float32) + from_z[...].astype(jnp.float32)
    fill = jnp.zeros((grad.shape[1] - CHUNK, LANES), jnp.float32)
    grad[...] = jnp.concatenate([done, fill], axis=0).T
    w.arrived(t_fin, fin_in)
    for n in range(capacity):
        finish(n, 1 - core, fin_in[n].astype(jnp.float32))
    w.finish()


def step_call(links, occupancy, features, cotangent, shard):
    live, group = LIVE, links.shape[1]
    capacity, voxels, channels = features.shape[1:]
    spatial, half = group // capacity, voxels // 2
    rest = CHUNK - CUT
    copies = 8 * 6 + 9 + 2 * live

    def buffer(*shape):
        return pltpu.VMEM(shape, jnp.bfloat16)

    def wide(*shape):
        return pltpu.VMEM(shape, jnp.float32)

    def ring(*shape):
        return [buffer(2, *shape, LANES)] * 3

    def scalars(*shape):
        return pltpu.SMEM(shape, jnp.int32)

    block = (capacity, voxels, channels)
    flops = 3 * 2 * live * voxels * 27 * channels * LANES
    return pl.pallas_call(
        step_kernel,
        out_shape=(
            jax.ShapeDtypeStruct(features.shape, jnp.bfloat16),
            jax.ShapeDtypeStruct((LANES, 3 * LANES), jnp.float32),
        ),
        in_specs=[SMEM_SPEC] + [VMEM_SPEC] * 4,
        out_specs=(VMEM_SPEC,) * 2,
        scratch_shapes=[
            buffer(CHUNK, LANES),
            buffer(spatial, capacity, voxels, LANES),
            wide(group, voxels, LANES),
            scalars(live, 27),
            scalars(live),
            scalars(group + 1),
            scalars(live),
            scalars(group),
            scalars(group),
            buffer(2, 4, 4, CHUNK, LANES),
            buffer(spatial, *block),
            buffer(spatial, capacity, voxels, LANES),
            wide(live + 1, 64, 8, channels),
            buffer(9, live, 10, 64, channels),
            buffer(live, voxels, LANES),
            buffer(LANES, live * voxels),
            wide(27 * channels + 16, LANES),
            buffer(27 * channels, LANES),
            wide(live + 1, 64, 8, LANES),
        ]
        + ring(4, CUT)
        + ring(4, rest)
        + [buffer(2, 4, CUT, LANES), buffer(2, 4, rest, LANES)]
        + ring(CUT)
        + ring(rest)
        + [
            buffer(2, CHUNK, LANES),
            buffer(CHUNK, LANES),
            buffer(live, 2, half, channels),
            buffer(live, half, channels),
            wide(live + 1, half, channels),
            buffer(live, half, channels),
            buffer(live + 1, half, channels),
            buffer(capacity, half, channels),
            buffer(capacity, half, channels),
            pltpu.SemaphoreType.DMA((2,)),
            pltpu.SemaphoreType.DMA((copies,)),
            pltpu.SemaphoreType.DMA((copies,)),
        ],
        compiler_params=pltpu.CompilerParams(
            collective_id=0, has_side_effects=True, vmem_limit_bytes=VMEM_BYTES
        ),
        cost_estimate=pl.CostEstimate(flops=flops, bytes_accessed=10**7, transcendentals=10**6),
    )(links, occupancy, features, cotangent, shard)


def body(features, cotangent, weight, occupancy, neighbours, first_moment, second_moment):
    input_grad, summed = step_call(neighbours, occupancy, features, cotangent, weight)
    scaled = summed[: first_moment.shape[1], : first_moment.shape[0]] / 64.0
    new_first = 0.9 * first_moment.T + 0.1 * scaled
    new_second = 0.999 * second_moment.T + 0.001 * scaled * scaled
    return input_grad, new_first.T, new_second.T


def solution(mesh):
    return jax.shard_map(
        body,
        mesh=mesh,
        in_specs=(
            P("dp", "space", None, None),
            P("dp", "space", None, None),
            P("dp", None),
            P("dp", None, None),
            P("dp", None, None),
            P("dp", "space"),
            P("dp", "space"),
        ),
        out_specs=(P("dp", "space", None, None), P("dp", "space"), P("dp", "space")),
        check_vma=False,
    )
```

```python
import jax
import jax.numpy as jnp
from jax import lax
from jax.experimental import pallas as pl
from jax.experimental.pallas import tpu as pltpu
from jax.sharding import PartitionSpec as P

LIVE = 4
LANES = 128
CHUNK = 336
CUT = 176
MESH = pl.DeviceIdType.MESH
VMEM_BYTES = 62 * 1024 * 1024


def fill_regions(table, blocks, regions, live):
    channels = blocks.shape[-1]
    row = lax.broadcasted_iota(jnp.int32, (1, 8, channels), 1)

    def plane(step, carry):
        r = step // 10
        i = step % 10
        first = jnp.where(i == 0, 0, jnp.where(i == 9, 2, 1))
        source = (i + 7) % 8
        code = 9 * first
        for c in range(3):
            pieces = []
            for second, start, count in ((0, 7, 1), (1, 0, 8), (2, 0, 1)):
                where = pl.ds(source * 8 + start, count)
                values = blocks[table[r, code + 3 * second + 1], where]
                if c != 1:
                    edge = blocks[table[r, code + 3 * second + c], where]
                    values = jnp.where(row == (7 if c == 0 else 0), edge, values)
                    values = pltpu.roll(values, 1 if c == 0 else 7, 1)
                pieces.append(values)
            line = jnp.concatenate(pieces, axis=0)
            for b in range(3):
                regions[3 * b + c, r, i] = (
                    line[b : b + 8].reshape(64, channels).astype(jnp.bfloat16)
                )
        return carry

    lax.fori_loop(0, live * 10, plane, 0)


def shifted_rows(regions, block, k, channels):
    a, bc = k // 9, k % 9
    return regions[bc, block, a : a + 8].reshape(512, channels)


SMEM_SPEC = pl.BlockSpec(memory_space=pltpu.SMEM)
VMEM_SPEC = pl.BlockSpec(memory_space=pltpu.VMEM)


class Wires:
    def __init__(self, send_sem, recv_sem):
        self.send_sem, self.recv_sem = send_sem, recv_sem
        dp, space = lax.axis_index("dp"), lax.axis_index("space")
        self.x, self.y, self.z = dp // 8, dp // 2 % 4, dp % 2
        self.chip, self.core = space // 2, space % 2
        self.started = []
        self.count = 0

    def at(self, x=None, y=None, z=None, chip=None, core=None):
        x, y, z = self.x if x is None else x, self.y if y is None else y, self.z if z is None else z
        chip, core = self.chip if chip is None else chip, self.core if core is None else core
        return (x * 8 + y * 2 + z, chip * 2 + core)

    def step(self, axis, by):
        return self.at(**{axis: (getattr(self, axis) + by) % 4})

    def greet(self, others):
        barrier = pltpu.get_barrier_semaphore()
        for other in others:
            pl.semaphore_signal(barrier, inc=1, device_id=other, device_id_type=MESH)

    def met(self, others):
        pl.semaphore_wait(pltpu.get_barrier_semaphore(), len(others))

    def everyone(self):
        return (
            [self.step(axis, by) for axis in ("x", "y") for by in (1, 3)]
            + [self.at(z=1 - self.z), self.at(chip=1 - self.chip), self.at(core=1 - self.core)]
            + [self.at(chip=1 - self.chip, core=1 - self.core)]
        )

    def ticket(self):
        self.count += 1
        return self.count - 1

    def send(self, ticket, source, target, other):
        copy = pltpu.make_async_remote_copy(
            source,
            target,
            self.send_sem.at[ticket],
            self.recv_sem.at[ticket],
            device_id=other,
            device_id_type=MESH,
        )
        copy.start()
        self.started.append(copy)

    def arrived(self, ticket, landing):
        pltpu.make_async_remote_copy(
            landing,
            landing,
            self.send_sem.at[ticket],
            self.recv_sem.at[ticket],
            device_id=self.at(core=1 - self.core),
            device_id_type=MESH,
        ).wait_recv()

    def finish(self):
        for copy in self.started:
            copy.wait_send()
        self.started = []


class RingGather:
    def __init__(self, wires, axis, block):
        self.wires, self.axis, self.block = wires, axis, block
        self.q = getattr(wires, axis)
        self.tickets = [wires.ticket() for _ in range(6)]

    def start(self):
        t, q = self.tickets, self.q
        right, left = self.wires.step(self.axis, 1), self.wires.step(self.axis, 3)
        for ticket, half, other in ((t[0], 0, right), (t[1], 1, left), (t[2], 1, right), (t[3], 0, left)):
            mine = self.block(q, half)
            self.wires.send(ticket, mine, mine, other)

    def forward(self):
        t, q = self.tickets, self.q
        right, left = self.wires.step(self.axis, 1), self.wires.step(self.axis, 3)
        for ticket, into, half, source, other in (
            (t[0], t[4], 0, (q + 3) % 4, right),
            (t[1], t[5], 1, (q + 1) % 4, left),
        ):
            piece = self.block(source, half)
            self.wires.arrived(ticket, piece)
            self.wires.send(into, piece, piece, other)

    def end(self):
        t, q = self.tickets, self.q
        self.wires.arrived(t[2], self.block((q + 3) % 4, 1))
        self.wires.arrived(t[3], self.block((q + 1) % 4, 0))
        self.wires.arrived(t[4], self.block((q + 2) % 4, 0))
        self.wires.arrived(t[5], self.block((q + 2) % 4, 1))


class RingReduce:
    def __init__(self, wires, axis, block, near, far_left, far_right):
        self.wires, self.axis, self.block = wires, axis, block
        self.near, self.far = near, (far_left, far_right)
        self.q = getattr(wires, axis)
        self.tickets = [wires.ticket() for _ in range(6)]

    def start(self):
        w, t, q = self.wires, self.tickets, self.q
        right, left = w.step(self.axis, 1), w.step(self.axis, 3)
        w.send(t[0], self.block((q + 2) % 4, 0), self.near.at[0], right)
        w.send(t[1], self.block((q + 2) % 4, 1), self.near.at[1], left)
        w.send(t[2], self.block((q + 1) % 4, 1), self.far[0].at[1], right)
        w.send(t[3], self.block((q + 3) % 4, 0), self.far[1].at[0], left)

    def forward(self):
        w, t, q = self.wires, self.tickets, self.q
        right, left = w.step(self.axis, 1), w.step(self.axis, 3)
        for half, target, other in ((0, (q + 1) % 4, right), (1, (q + 3) % 4, left)):
            w.arrived(t[half], self.near.at[half])
            own = self.block(target, half)[...].astype(jnp.float32)
            self.near[half] = (self.near[half].astype(jnp.float32) + own).astype(jnp.bfloat16)
            w.send(t[4 + half], self.near.at[half], self.far[half].at[half], other)

    def end(self, out):
        w, t, q = self.wires, self.tickets, self.q
        w.arrived(t[2], self.far[0].at[1])
        w.arrived(t[3], self.far[1].at[0])
        w.arrived(t[4], self.far[0].at[0])
        w.arrived(t[5], self.far[1].at[1])
        for half in range(2):
            total = self.block(q, half)[...].astype(jnp.float32)
            total = total + self.far[0][half].astype(jnp.float32)
            total = total + self.far[1][half].astype(jnp.float32)
            out[half] = total.astype(out.dtype)


def read_links(links, chip, table, slots, place, order, inward, onward):
    group = links.shape[1]
    alive = [(links[0, s, 13] >= 0).astype(jnp.int32) for s in range(group)]
    near = [(chip == s // (group // 2)).astype(jnp.int32) for s in range(group)]
    others = sum(a * (1 - n) for a, n in zip(alive, near))
    rank, counts, position = [], [0, 0], []
    total = 0
    for s in range(group):
        side = s // (group // 2)
        rank.append(total)
        position.append(counts[side] + near[s] * others)
        place[s + 1] = jnp.where(alive[s] > 0, jnp.minimum(total, LIVE), LIVE)
        inward[s] = jnp.where(alive[s] > 0, jnp.minimum(counts[side], LIVE), LIVE)
        onward[s] = jnp.where(alive[s] > 0, jnp.minimum(position[s], LIVE), LIVE)
        total = total + alive[s]
        counts[side] = counts[side] + alive[s]
    place[0] = LIVE
    for r in range(LIVE):
        slots[r] = sum(jnp.where(rank[s] == r, alive[s] * s, 0) for s in range(group))
        turn = sum(jnp.where(position[s] == r, alive[s] * rank[s], 0) for s in range(group))
        order[r] = jnp.minimum(turn, LIVE - 1)

    def code_of(code, carry):
        for r in range(LIVE):
            table[r, code] = place[links[0, slots[r], code] + 1]
        return carry

    lax.fori_loop(0, 27, code_of, 0)


def lanes_from(values, start):
    return pltpu.roll(values, (values.shape[1] - start) % values.shape[1], 1)[:, :LANES]


def step_kernel(
    links, occupancy, features, cotangent, shard, input_grad, grad,
    rows, cot_own, mask, table, slots, place, order, inward, onward,
    parts, feat, cot, blocks, regions, delta_t, stage, weight, weight_t, thin,
    a_near, a_left, a_right, b_near, b_left, b_right, a_mid, b_mid,
    c_near, c_left, c_right, d_near, d_left, d_right, last, from_z,
    halves, inbox, chip_sum, z_out, z_in, fin_out, fin_in,
    local_sem, send_sem, recv_sem,
):
    live, group = LIVE, links.shape[1]
    capacity, voxels, channels = features.shape[1:]
    spatial = group // capacity
    width = channels // spatial
    rows_of = shard.shape[0]
    half = voxels // 2
    w = Wires(send_sem, recv_sem)
    x, y, z, chip, core = w.x, w.y, w.z, w.chip, w.core
    me, over, beside = chip * 2 + core, (1 - chip) * 2 + core, chip * 2 + 1 - core
    across = (1 - chip) * 2 + 1 - core
    to_over, to_beside = w.at(chip=1 - chip), w.at(core=1 - core)
    to_across = w.at(chip=1 - chip, core=1 - core)
    t_z, t_over, t_beside, t_across = (w.ticket() for _ in range(4))
    c_over, c_beside, c_across = (w.ticket() for _ in range(3))
    first_a = RingGather(w, "x", lambda q, h: parts.at[h, q, y, :CUT])
    first_b = RingGather(w, "y", lambda q, h: parts.at[h, x, q, CUT:])
    last_a = RingGather(w, "y", lambda q, h: parts.at[h, :, q, :CUT])
    last_b = RingGather(w, "x", lambda q, h: parts.at[h, q, :, CUT:])
    sum_a = RingReduce(w, "y", lambda q, h: parts.at[h, :, q, :CUT], a_near, a_left, a_right)
    sum_b = RingReduce(w, "x", lambda q, h: parts.at[h, q, :, CUT:], b_near, b_left, b_right)
    end_a = RingReduce(w, "x", lambda q, h: a_mid.at[h, q], c_near, c_left, c_right)
    end_b = RingReduce(w, "y", lambda q, h: b_mid.at[h, q], d_near, d_left, d_right)
    t_out, t_fin = w.ticket(), w.ticket()
    t_core = [w.ticket() for _ in range(live)]
    t_chip = [w.ticket() for _ in range(live)]

    w.greet(w.everyone())
    rows[CHUNK - 16 :] = jnp.zeros((16, LANES), jnp.bfloat16)
    start = (spatial - me) % spatial * width
    turned = pltpu.roll(shard[...].astype(jnp.float32), start, 1)[:, :LANES]
    lane = lax.broadcasted_iota(jnp.int32, turned.shape, 1)
    rows[:rows_of] = jnp.where(lane < width, turned, 0.0).astype(jnp.bfloat16)
    w.met(w.everyone())
    w.send(t_z, rows, parts.at[z, x, y], w.at(z=1 - z))
    w.send(t_over, features.at[0], feat.at[me], to_over)
    w.send(t_beside, features.at[0], feat.at[me], to_beside)
    keep = [
        pltpu.make_async_copy(rows, parts.at[z, x, y], local_sem.at[0]),
        pltpu.make_async_copy(features.at[0], feat.at[me], local_sem.at[1]),
    ]
    for copy in keep:
        copy.start()
    read_links(links, chip, table, slots, place, order, inward, onward)
    keep[0].wait()
    w.arrived(t_z, parts.at[1 - z, x, y])
    first_a.start()
    first_b.start()
    for s in range(spatial):
        for n in range(capacity):
            some = lanes_from(cotangent[0, n].astype(jnp.float32), s * width)
            cot_own[s, n] = some.T[:width].astype(jnp.bfloat16)
    cot[me] = cot_own[me]
    w.send(c_beside, cot_own.at[beside], cot.at[me], to_beside)
    held = occupancy[0].astype(jnp.float32)
    held = jnp.concatenate([held] * (LANES // group), axis=0).T
    for s in range(group):
        mask[s] = jnp.broadcast_to(held[:, s : s + 1], (voxels, LANES))
    first_a.forward()
    first_b.forward()
    first_a.end()
    first_b.end()
    last_a.start()
    last_b.start()
    w.arrived(t_over, feat.at[over])
    w.send(t_across, feat.at[over], feat.at[over], to_beside)
    w.send(c_over, cot_own.at[over], cot.at[me], to_over)
    w.send(c_across, cot_own.at[across], cot.at[me], to_across)
    last_a.forward()
    last_b.forward()
    keep[1].wait()
    w.arrived(t_beside, feat.at[beside])
    w.arrived(t_across, feat.at[across])

    for r in range(live):
        full = jnp.concatenate([mask[slots[r]]] * (channels // LANES), axis=1)
        field = feat[slots[r] // capacity, slots[r] % capacity].astype(jnp.float32)
        blocks[r] = (field * full).reshape(64, 8, channels)
    blocks[live] = jnp.zeros((64, 8, channels), jnp.float32)
    fill_regions(table, blocks, regions, live)
    last_a.end()
    last_b.end()
    for d in range(32):
        stage[rows_of * d : rows_of * d + CHUNK] = parts[d % 2, d // 8, d // 2 % 4].astype(
            jnp.float32
        )
    for k in range(27):
        some = stage[pl.ds(k, channels, stride=27), :]
        weight[k * channels : (k + 1) * channels] = some.astype(jnp.bfloat16)
        weight_t[:, k * channels : (k + 1) * channels] = some.T[:width].astype(jnp.bfloat16)
    w.arrived(c_over, cot.at[over])
    w.arrived(c_beside, cot.at[beside])
    w.arrived(c_across, cot.at[across])

    def forward_block(r):
        pre = jnp.zeros((width, voxels), jnp.float32)
        for ks in (range(g, min(g + 2, 27)) for g in range(0, 27, 2)):
            field = jnp.concatenate([shifted_rows(regions, r, k, channels) for k in ks], axis=1)
            lhs = weight_t[:, ks[0] * channels : (ks[-1] + 1) * channels]
            pre = pre + lax.dot_general(
                lhs, field, (((1,), (1,)), ((), ())), preferred_element_type=jnp.float32
            )
        gate = jax.nn.sigmoid(pre)
        value = cot[slots[r] // capacity, slots[r] % capacity].astype(jnp.float32)
        value = value * occupancy[0, pl.ds(slots[r], 1)].astype(jnp.float32)
        value = (value * gate * (1.0 + pre * (1.0 - gate))).astype(jnp.bfloat16)
        delta_t[:, r * voxels : (r + 1) * voxels] = value
        value = jnp.concatenate(
            [value.astype(jnp.float32), jnp.zeros((LANES - width, voxels), jnp.float32)], axis=0
        )
        thin[r] = value.T.reshape(64, 8, LANES)

    for r in range(live):
        forward_block(r)
    for k in range(27):
        field = jnp.concatenate(
            [shifted_rows(regions, r, k, channels) for r in range(live)], axis=0
        )
        part = jnp.dot(delta_t[...], field, preferred_element_type=jnp.float32)
        part = jnp.concatenate(
            [part, jnp.zeros((LANES - width, channels), jnp.float32)], axis=0
        )
        stage[pl.ds(k, channels, stride=27), :] = part.T
    w.finish()
    for d in range(32):
        parts[d % 2, d // 8, d // 2 % 4] = stage[rows_of * d : rows_of * d + CHUNK].astype(
            jnp.bfloat16
        )
    sum_a.start()
    sum_b.start()

    thin[live] = jnp.zeros((64, 8, LANES), jnp.float32)
    narrow = regions.at[:, :, :, :, :LANES]
    fill_regions(table, thin, narrow, live)

    chip_sum[live] = jnp.zeros((half, channels), jnp.float32)
    z_in[live] = jnp.zeros((half, channels), jnp.bfloat16)

    def back_block(j):
        r = order[j]
        out = jnp.zeros((voxels, channels), jnp.float32)
        for ks in (range(g, min(g + 4, 27)) for g in range(0, 27, 4)):
            lhs = jnp.concatenate([shifted_rows(narrow, r, 26 - k, LANES) for k in ks], axis=1)
            rhs = jnp.concatenate(
                [weight[k * channels : (k + 1) * channels] for k in ks], axis=1
            )
            out = out + lax.dot_general(
                lhs, rhs, (((1,), (1,)), ((), ())), preferred_element_type=jnp.float32
            )
        halves[j] = out.astype(jnp.bfloat16).reshape(2, half, channels)
        w.send(t_core[j], halves.at[j, 1 - core], inbox.at[j], to_beside)

    def join(j):
        w.arrived(t_core[j], inbox.at[j])
        value = halves[j, core].astype(jnp.float32) + inbox[j].astype(jnp.float32)
        chip_sum[j] = value
        z_out[j] = value.astype(jnp.bfloat16)
        w.send(t_chip[j], z_out.at[j], z_in.at[j], to_over)

    back_block(0)
    back_block(1)
    join(0)
    sum_a.forward()
    sum_b.forward()
    back_block(2)
    join(1)
    back_block(3)
    join(2)
    sum_a.end(a_mid)
    sum_b.end(b_mid)
    end_a.start()
    end_b.start()
    join(3)
    end_a.forward()
    end_b.forward()
    end_a.end(last.at[:, :CUT])
    end_b.end(last.at[:, CUT:])
    w.send(t_out, last.at[1 - z], from_z, w.at(z=1 - z))
    for j in range(live):
        w.arrived(t_chip[j], z_in.at[j])

    def whole(owner, n):
        s = owner * capacity + n
        return z_in[inward[s]].astype(jnp.float32) + chip_sum[onward[s]]

    def finish(n, part, value):
        span = pl.ds(pl.multiple_of(part * half, half), half)
        full = jnp.concatenate([mask[me * capacity + n, span]] * (channels // LANES), axis=1)
        value = cotangent[0, n, span].astype(jnp.float32) + full * value
        input_grad[0, n, span] = value.astype(jnp.bfloat16)

    for n in range(capacity):
        fin_out[n] = whole(beside, n).astype(jnp.bfloat16)
    w.send(t_fin, fin_out, fin_in, to_beside)
    for n in range(capacity):
        finish(n, core, whole(me, n))
    w.arrived(t_out, from_z)
    done = last[z].astype(jnp.float32) + from_z[...].astype(jnp.float32)
    fill = jnp.zeros((grad.shape[1] - CHUNK, LANES), jnp.float32)
    grad[...] = jnp.concatenate([done, fill], axis=0).T
    w.arrived(t_fin, fin_in)
    for n in range(capacity):
        finish(n, 1 - core, fin_in[n].astype(jnp.float32))
    w.finish()


def step_call(links, occupancy, features, cotangent, shard):
    live, group = LIVE, links.shape[1]
    capacity, voxels, channels = features.shape[1:]
    spatial, half = group // capacity, voxels // 2
    rest = CHUNK - CUT
    copies = 8 * 6 + 9 + 2 * live

    def buffer(*shape):
        return pltpu.VMEM(shape, jnp.bfloat16)

    def wide(*shape):
        return pltpu.VMEM(shape, jnp.float32)

    def ring(*shape):
        return [buffer(2, *shape, LANES)] * 3

    def scalars(*shape):
        return pltpu.SMEM(shape, jnp.int32)

    block = (capacity, voxels, channels)
    flops = 3 * 2 * live * voxels * 27 * channels * LANES
    return pl.pallas_call(
        step_kernel,
        out_shape=(
            jax.ShapeDtypeStruct(features.shape, jnp.bfloat16),
            jax.ShapeDtypeStruct((LANES, 3 * LANES), jnp.float32),
        ),
        in_specs=[SMEM_SPEC] + [VMEM_SPEC] * 4,
        out_specs=(VMEM_SPEC,) * 2,
        scratch_shapes=[
            buffer(CHUNK, LANES),
            buffer(spatial, capacity, channels // spatial, voxels),
            wide(group, voxels, LANES),
            scalars(live, 27),
            scalars(live),
            scalars(group + 1),
            scalars(live),
            scalars(group),
            scalars(group),
            buffer(2, 4, 4, CHUNK, LANES),
            buffer(spatial, *block),
            buffer(spatial, capacity, channels // spatial, voxels),
            wide(live + 1, 64, 8, channels),
            buffer(9, live, 10, 64, channels),
            buffer(channels // spatial, live * voxels),
            wide(27 * channels + 16, LANES),
            buffer(27 * channels, LANES),
            buffer(channels // spatial, 27 * channels),
            wide(live + 1, 64, 8, LANES),
        ]
        + ring(4, CUT)
        + ring(4, rest)
        + [buffer(2, 4, CUT, LANES), buffer(2, 4, rest, LANES)]
        + ring(CUT)
        + ring(rest)
        + [
            buffer(2, CHUNK, LANES),
            buffer(CHUNK, LANES),
            buffer(live, 2, half, channels),
            buffer(live, half, channels),
            wide(live + 1, half, channels),
            buffer(live, half, channels),
            buffer(live + 1, half, channels),
            buffer(capacity, half, channels),
            buffer(capacity, half, channels),
            pltpu.SemaphoreType.DMA((2,)),
            pltpu.SemaphoreType.DMA((copies,)),
            pltpu.SemaphoreType.DMA((copies,)),
        ],
        compiler_params=pltpu.CompilerParams(
            collective_id=0, has_side_effects=True, vmem_limit_bytes=VMEM_BYTES
        ),
        cost_estimate=pl.CostEstimate(flops=flops, bytes_accessed=10**7, transcendentals=10**6),
    )(links, occupancy, features, cotangent, shard)


def body(features, cotangent, weight, occupancy, neighbours, first_moment, second_moment):
    input_grad, summed = step_call(neighbours, occupancy, features, cotangent, weight)
    scaled = summed[: first_moment.shape[1], : first_moment.shape[0]] / 64.0
    new_first = 0.9 * first_moment.T + 0.1 * scaled
    new_second = 0.999 * second_moment.T + 0.001 * scaled * scaled
    return input_grad, new_first.T, new_second.T


def solution(mesh):
    return jax.shard_map(
        body,
        mesh=mesh,
        in_specs=(
            P("dp", "space", None, None),
            P("dp", "space", None, None),
            P("dp", None),
            P("dp", None, None),
            P("dp", None, None),
            P("dp", "space"),
            P("dp", "space"),
        ),
        out_specs=(P("dp", "space", None, None), P("dp", "space"), P("dp", "space")),
        check_vma=False,
    )
```

```python
import jax
import jax.numpy as jnp
from jax import lax
from jax.experimental import pallas as pl
from jax.experimental.pallas import tpu as pltpu
from jax.sharding import PartitionSpec as P

LIVE = 4
LANES = 128
CHUNK = 336
CUT = 176
MESH = pl.DeviceIdType.MESH
VMEM_BYTES = 62 * 1024 * 1024


def fill_regions(table, blocks, regions, live):
    channels = blocks.shape[-1]
    row = lax.broadcasted_iota(jnp.int32, (1, 8, channels), 1)

    def plane(step, carry):
        r = step // 10
        i = step % 10
        first = jnp.where(i == 0, 0, jnp.where(i == 9, 2, 1))
        source = (i + 7) % 8
        code = 9 * first
        for c in range(3):
            pieces = []
            for second, start, count in ((0, 7, 1), (1, 0, 8), (2, 0, 1)):
                where = pl.ds(source * 8 + start, count)
                values = blocks[table[r, code + 3 * second + 1], where]
                if c != 1:
                    edge = blocks[table[r, code + 3 * second + c], where]
                    values = jnp.where(row == (7 if c == 0 else 0), edge, values)
                    values = pltpu.roll(values, 1 if c == 0 else 7, 1)
                pieces.append(values)
            line = jnp.concatenate(pieces, axis=0)
            for b in range(3):
                regions[3 * b + c, r, i] = (
                    line[b : b + 8].reshape(64, channels).astype(jnp.bfloat16)
                )
        return carry

    lax.fori_loop(0, live * 10, plane, 0)


def shifted_rows(regions, block, k, channels):
    a, bc = k // 9, k % 9
    return regions[bc, block, a : a + 8].reshape(512, channels)


SMEM_SPEC = pl.BlockSpec(memory_space=pltpu.SMEM)
VMEM_SPEC = pl.BlockSpec(memory_space=pltpu.VMEM)


class Wires:
    def __init__(self, send_sem, recv_sem):
        self.send_sem, self.recv_sem = send_sem, recv_sem
        dp, space = lax.axis_index("dp"), lax.axis_index("space")
        self.x, self.y, self.z = dp // 8, dp // 2 % 4, dp % 2
        self.chip, self.core = space // 2, space % 2
        self.started = []
        self.count = 0

    def at(self, x=None, y=None, z=None, chip=None, core=None):
        x, y, z = self.x if x is None else x, self.y if y is None else y, self.z if z is None else z
        chip, core = self.chip if chip is None else chip, self.core if core is None else core
        return (x * 8 + y * 2 + z, chip * 2 + core)

    def step(self, axis, by):
        return self.at(**{axis: (getattr(self, axis) + by) % 4})

    def greet(self, others):
        barrier = pltpu.get_barrier_semaphore()
        for other in others:
            pl.semaphore_signal(barrier, inc=1, device_id=other, device_id_type=MESH)

    def met(self, others):
        pl.semaphore_wait(pltpu.get_barrier_semaphore(), len(others))

    def everyone(self):
        return (
            [self.step(axis, by) for axis in ("x", "y") for by in (1, 3)]
            + [self.at(z=1 - self.z), self.at(chip=1 - self.chip), self.at(core=1 - self.core)]
            + [self.at(chip=1 - self.chip, core=1 - self.core)]
        )

    def ticket(self):
        self.count += 1
        return self.count - 1

    def send(self, ticket, source, target, other):
        copy = pltpu.make_async_remote_copy(
            source,
            target,
            self.send_sem.at[ticket],
            self.recv_sem.at[ticket],
            device_id=other,
            device_id_type=MESH,
        )
        copy.start()
        self.started.append(copy)

    def arrived(self, ticket, landing):
        pltpu.make_async_remote_copy(
            landing,
            landing,
            self.send_sem.at[ticket],
            self.recv_sem.at[ticket],
            device_id=self.at(core=1 - self.core),
            device_id_type=MESH,
        ).wait_recv()

    def finish(self):
        for copy in self.started:
            copy.wait_send()
        self.started = []


class RingGather:
    def __init__(self, wires, axis, block):
        self.wires, self.axis, self.block = wires, axis, block
        self.q = getattr(wires, axis)
        self.base = [wires.ticket() for _ in range(6)][0]

    def start(self, h):
        w, mine = self.wires, self.block(self.q, h)
        w.send(self.base + 3 * h, mine, mine, w.step(self.axis, 1 + 2 * h))
        w.send(self.base + 3 * h + 1, mine, mine, w.step(self.axis, 3 + 2 * h))

    def forward(self, h):
        w, piece = self.wires, self.block((self.q + 3 + 2 * h) % 4, h)
        w.arrived(self.base + 3 * h, piece)
        w.send(self.base + 3 * h + 2, piece, piece, w.step(self.axis, 1 + 2 * h))

    def end(self, h):
        w, q = self.wires, self.q
        w.arrived(self.base + 3 * h + 1, self.block((q + 1 + 2 * h) % 4, h))
        w.arrived(self.base + 3 * h + 2, self.block((q + 2) % 4, h))


class RingReduce:
    def __init__(self, wires, axis, block, near, direct, relay):
        self.wires, self.axis, self.block = wires, axis, block
        self.near, self.direct, self.relay = near, direct, relay
        self.q = getattr(wires, axis)
        self.base = [wires.ticket() for _ in range(6)][0]

    def start(self, h):
        w, q, t = self.wires, self.q, self.base + 3 * h
        w.send(t, self.block((q + 2) % 4, h), self.near.at[h], w.step(self.axis, 1 + 2 * h))
        beyond = self.block((q + 3 + 2 * h) % 4, h)
        w.send(t + 1, beyond, self.direct.at[h], w.step(self.axis, 3 + 2 * h))

    def forward(self, h):
        w, q, t = self.wires, self.q, self.base + 3 * h
        w.arrived(t, self.near.at[h])
        own = self.block((q + 1 + 2 * h) % 4, h)[...].astype(jnp.float32)
        self.near[h] = (self.near[h].astype(jnp.float32) + own).astype(jnp.bfloat16)
        w.send(t + 2, self.near.at[h], self.relay.at[h], w.step(self.axis, 1 + 2 * h))

    def end(self, h, out):
        w, t = self.wires, self.base + 3 * h
        w.arrived(t + 1, self.direct.at[h])
        w.arrived(t + 2, self.relay.at[h])
        total = self.block(self.q, h)[...].astype(jnp.float32)
        total = total + self.direct[h].astype(jnp.float32)
        total = total + self.relay[h].astype(jnp.float32)
        out[h] = total.astype(out.dtype)


def read_links(links, chip, table, slots, place, order, inward, onward):
    group = links.shape[1]
    alive = [(links[0, s, 13] >= 0).astype(jnp.int32) for s in range(group)]
    near = [(chip == s // (group // 2)).astype(jnp.int32) for s in range(group)]
    others = sum(a * (1 - n) for a, n in zip(alive, near))
    rank, counts, position = [], [0, 0], []
    total = 0
    for s in range(group):
        side = s // (group // 2)
        rank.append(total)
        position.append(counts[side] + near[s] * others)
        place[s + 1] = jnp.where(alive[s] > 0, jnp.minimum(total, LIVE), LIVE)
        inward[s] = jnp.where(alive[s] > 0, jnp.minimum(counts[side], LIVE), LIVE)
        onward[s] = jnp.where(alive[s] > 0, jnp.minimum(position[s], LIVE), LIVE)
        total = total + alive[s]
        counts[side] = counts[side] + alive[s]
    place[0] = LIVE
    for r in range(LIVE):
        slots[r] = sum(jnp.where(rank[s] == r, alive[s] * s, 0) for s in range(group))
        turn = sum(jnp.where(position[s] == r, alive[s] * rank[s], 0) for s in range(group))
        order[r] = jnp.minimum(turn, LIVE - 1)

    def code_of(code, carry):
        for r in range(LIVE):
            table[r, code] = place[links[0, slots[r], code] + 1]
        return carry

    lax.fori_loop(0, 27, code_of, 0)


def lanes_from(values, start):
    return pltpu.roll(values, (values.shape[1] - start) % values.shape[1], 1)[:, :LANES]


def step_kernel(
    links, occupancy, features, cotangent, shard, input_grad, grad,
    rows, cot_own, mask, table, slots, place, order, inward, onward,
    parts, feat, cot, blocks, regions, delta_t, stage, weight, weight_t, thin,
    a_near, a_direct, a_relay, b_near, b_direct, b_relay, a_mid, b_mid,
    c_near, c_direct, c_relay, d_near, d_direct, d_relay, last, from_z,
    halves, inbox, chip_sum, z_out, z_in, fin_out, fin_in,
    local_sem, send_sem, recv_sem,
):
    live, group = LIVE, links.shape[1]
    capacity, voxels, channels = features.shape[1:]
    spatial = group // capacity
    width = channels // spatial
    rows_of = shard.shape[0]
    half = voxels // 2
    w = Wires(send_sem, recv_sem)
    x, y, z, chip, core = w.x, w.y, w.z, w.chip, w.core
    me, over, beside = chip * 2 + core, (1 - chip) * 2 + core, chip * 2 + 1 - core
    across = (1 - chip) * 2 + 1 - core
    to_over, to_beside = w.at(chip=1 - chip), w.at(core=1 - core)
    to_across = w.at(chip=1 - chip, core=1 - core)
    t_z, t_over, t_beside, t_across = (w.ticket() for _ in range(4))
    c_over, c_beside, c_across = (w.ticket() for _ in range(3))
    first_a = RingGather(w, "x", lambda q, h: parts.at[h, q, y, :CUT])
    first_b = RingGather(w, "y", lambda q, h: parts.at[h, x, q, CUT:])
    last_a = RingGather(w, "y", lambda q, h: parts.at[h, :, q, :CUT])
    last_b = RingGather(w, "x", lambda q, h: parts.at[h, q, :, CUT:])
    sum_a = RingReduce(w, "y", lambda q, h: parts.at[h, :, q, :CUT], a_near, a_direct, a_relay)
    sum_b = RingReduce(w, "x", lambda q, h: parts.at[h, q, :, CUT:], b_near, b_direct, b_relay)
    end_a = RingReduce(w, "x", lambda q, h: a_mid.at[h, q], c_near, c_direct, c_relay)
    end_b = RingReduce(w, "y", lambda q, h: b_mid.at[h, q], d_near, d_direct, d_relay)
    t_out, t_fin = w.ticket(), w.ticket()
    t_core = [w.ticket() for _ in range(live)]
    t_chip = [w.ticket() for _ in range(live)]

    w.greet(w.everyone())
    rows[CHUNK - 16 :] = jnp.zeros((16, LANES), jnp.bfloat16)
    start = (spatial - me) % spatial * width
    turned = pltpu.roll(shard[...].astype(jnp.float32), start, 1)[:, :LANES]
    lane = lax.broadcasted_iota(jnp.int32, turned.shape, 1)
    rows[:rows_of] = jnp.where(lane < width, turned, 0.0).astype(jnp.bfloat16)
    w.met(w.everyone())
    rounds = (z, 1 - z)
    w.send(t_z, rows, parts.at[z, x, y], w.at(z=1 - z))
    w.send(t_over, features.at[0], feat.at[me], to_over)
    keep = [
        pltpu.make_async_copy(rows, parts.at[z, x, y], local_sem.at[0]),
        pltpu.make_async_copy(features.at[0], feat.at[me], local_sem.at[1]),
    ]
    for copy in keep:
        copy.start()
    keep[0].wait()
    first_a.start(z)
    first_b.start(z)
    w.send(t_beside, features.at[0], feat.at[me], to_beside)
    read_links(links, chip, table, slots, place, order, inward, onward)
    first_a.forward(z)
    first_b.forward(z)
    w.arrived(t_z, parts.at[1 - z, x, y])
    first_a.start(1 - z)
    first_b.start(1 - z)
    for s in range(spatial):
        for n in range(capacity):
            some = lanes_from(cotangent[0, n].astype(jnp.float32), s * width)
            cot_own[s, n] = some.T[:width].astype(jnp.bfloat16)
    cot[me] = cot_own[me]
    w.send(c_beside, cot_own.at[beside], cot.at[me], to_beside)
    first_a.end(z)
    first_b.end(z)
    last_a.start(z)
    last_b.start(z)
    first_a.forward(1 - z)
    first_b.forward(1 - z)
    held = occupancy[0].astype(jnp.float32)
    held = jnp.concatenate([held] * (LANES // group), axis=0).T
    for s in range(group):
        mask[s] = jnp.broadcast_to(held[:, s : s + 1], (voxels, LANES))
    last_a.forward(z)
    last_b.forward(z)
    first_a.end(1 - z)
    first_b.end(1 - z)
    last_a.start(1 - z)
    last_b.start(1 - z)
    w.arrived(t_over, feat.at[over])
    w.send(t_across, feat.at[over], feat.at[over], to_beside)
    w.send(c_over, cot_own.at[over], cot.at[me], to_over)
    w.send(c_across, cot_own.at[across], cot.at[me], to_across)
    last_a.forward(1 - z)
    last_b.forward(1 - z)
    keep[1].wait()
    w.arrived(t_beside, feat.at[beside])
    w.arrived(t_across, feat.at[across])

    for r in range(live):
        full = jnp.concatenate([mask[slots[r]]] * (channels // LANES), axis=1)
        field = feat[slots[r] // capacity, slots[r] % capacity].astype(jnp.float32)
        blocks[r] = (field * full).reshape(64, 8, channels)
    blocks[live] = jnp.zeros((64, 8, channels), jnp.float32)
    fill_regions(table, blocks, regions, live)
    for h in rounds:
        last_a.end(h)
        last_b.end(h)
    for d in range(32):
        stage[rows_of * d : rows_of * d + CHUNK] = parts[d % 2, d // 8, d // 2 % 4].astype(
            jnp.float32
        )
    for k in range(27):
        some = stage[pl.ds(k, channels, stride=27), :]
        weight[k * channels : (k + 1) * channels] = some.astype(jnp.bfloat16)
        weight_t[:, k * channels : (k + 1) * channels] = some.T[:width].astype(jnp.bfloat16)
    w.arrived(c_over, cot.at[over])
    w.arrived(c_beside, cot.at[beside])
    w.arrived(c_across, cot.at[across])

    def forward_block(r):
        pre = jnp.zeros((width, voxels), jnp.float32)
        for ks in (range(g, min(g + 2, 27)) for g in range(0, 27, 2)):
            field = jnp.concatenate([shifted_rows(regions, r, k, channels) for k in ks], axis=1)
            lhs = weight_t[:, ks[0] * channels : (ks[-1] + 1) * channels]
            pre = pre + lax.dot_general(
                lhs, field, (((1,), (1,)), ((), ())), preferred_element_type=jnp.float32
            )
        gate = jax.nn.sigmoid(pre)
        value = cot[slots[r] // capacity, slots[r] % capacity].astype(jnp.float32)
        value = value * occupancy[0, pl.ds(slots[r], 1)].astype(jnp.float32)
        value = (value * gate * (1.0 + pre * (1.0 - gate))).astype(jnp.bfloat16)
        delta_t[:, r * voxels : (r + 1) * voxels] = value
        value = jnp.concatenate(
            [value.astype(jnp.float32), jnp.zeros((LANES - width, voxels), jnp.float32)], axis=0
        )
        thin[r] = value.T.reshape(64, 8, LANES)

    for r in range(live):
        forward_block(r)
    for k in range(27):
        field = jnp.concatenate(
            [shifted_rows(regions, r, k, channels) for r in range(live)], axis=0
        )
        part = jnp.dot(delta_t[...], field, preferred_element_type=jnp.float32)
        part = jnp.concatenate(
            [part, jnp.zeros((LANES - width, channels), jnp.float32)], axis=0
        )
        stage[pl.ds(k, channels, stride=27), :] = part.T
    w.finish()
    for d in range(32):
        parts[d % 2, d // 8, d // 2 % 4] = stage[rows_of * d : rows_of * d + CHUNK].astype(
            jnp.bfloat16
        )
    for h in rounds[::-1]:
        sum_a.start(h)
        sum_b.start(h)

    thin[live] = jnp.zeros((64, 8, LANES), jnp.float32)
    narrow = regions.at[:, :, :, :, :LANES]
    fill_regions(table, thin, narrow, live)

    chip_sum[live] = jnp.zeros((half, channels), jnp.float32)
    z_in[live] = jnp.zeros((half, channels), jnp.bfloat16)

    def back_block(j):
        r = order[j]
        out = jnp.zeros((voxels, channels), jnp.float32)
        for ks in (range(g, min(g + 4, 27)) for g in range(0, 27, 4)):
            lhs = jnp.concatenate([shifted_rows(narrow, r, 26 - k, LANES) for k in ks], axis=1)
            rhs = jnp.concatenate(
                [weight[k * channels : (k + 1) * channels] for k in ks], axis=1
            )
            out = out + lax.dot_general(
                lhs, rhs, (((1,), (1,)), ((), ())), preferred_element_type=jnp.float32
            )
        halves[j] = out.astype(jnp.bfloat16).reshape(2, half, channels)
        w.send(t_core[j], halves.at[j, 1 - core], inbox.at[j], to_beside)

    def join(j):
        w.arrived(t_core[j], inbox.at[j])
        value = halves[j, core].astype(jnp.float32) + inbox[j].astype(jnp.float32)
        chip_sum[j] = value
        z_out[j] = value.astype(jnp.bfloat16)
        w.send(t_chip[j], z_out.at[j], z_in.at[j], to_over)

    first, second = 1 - z, z
    back_block(0)
    sum_a.forward(first)
    sum_b.forward(first)
    back_block(1)
    join(0)
    sum_a.forward(second)
    sum_b.forward(second)
    back_block(2)
    join(1)
    sum_a.end(first, a_mid)
    sum_b.end(first, b_mid)
    end_a.start(first)
    end_b.start(first)
    back_block(3)
    join(2)
    sum_a.end(second, a_mid)
    sum_b.end(second, b_mid)
    end_a.start(second)
    end_b.start(second)
    end_a.forward(first)
    end_b.forward(first)
    join(3)
    end_a.end(first, last.at[:, :CUT])
    end_b.end(first, last.at[:, CUT:])
    w.send(t_out, last.at[1 - z], from_z, w.at(z=1 - z))
    end_a.forward(second)
    end_b.forward(second)
    end_a.end(second, last.at[:, :CUT])
    end_b.end(second, last.at[:, CUT:])
    for j in range(live):
        w.arrived(t_chip[j], z_in.at[j])

    def whole(owner, n):
        s = owner * capacity + n
        return z_in[inward[s]].astype(jnp.float32) + chip_sum[onward[s]]

    def finish(n, part, value):
        span = pl.ds(pl.multiple_of(part * half, half), half)
        full = jnp.concatenate([mask[me * capacity + n, span]] * (channels // LANES), axis=1)
        value = cotangent[0, n, span].astype(jnp.float32) + full * value
        input_grad[0, n, span] = value.astype(jnp.bfloat16)

    for n in range(capacity):
        fin_out[n] = whole(beside, n).astype(jnp.bfloat16)
    w.send(t_fin, fin_out, fin_in, to_beside)
    for n in range(capacity):
        finish(n, core, whole(me, n))
    w.arrived(t_out, from_z)
    done = last[z].astype(jnp.float32) + from_z[...].astype(jnp.float32)
    fill = jnp.zeros((grad.shape[1] - CHUNK, LANES), jnp.float32)
    grad[...] = jnp.concatenate([done, fill], axis=0).T
    w.arrived(t_fin, fin_in)
    for n in range(capacity):
        finish(n, 1 - core, fin_in[n].astype(jnp.float32))
    w.finish()


def step_call(links, occupancy, features, cotangent, shard):
    live, group = LIVE, links.shape[1]
    capacity, voxels, channels = features.shape[1:]
    spatial, half = group // capacity, voxels // 2
    rest = CHUNK - CUT
    copies = 8 * 6 + 9 + 2 * live

    def buffer(*shape):
        return pltpu.VMEM(shape, jnp.bfloat16)

    def wide(*shape):
        return pltpu.VMEM(shape, jnp.float32)

    def ring(*shape):
        return [buffer(2, *shape, LANES)] * 3

    def scalars(*shape):
        return pltpu.SMEM(shape, jnp.int32)

    block = (capacity, voxels, channels)
    flops = 3 * 2 * live * voxels * 27 * channels * LANES
    return pl.pallas_call(
        step_kernel,
        out_shape=(
            jax.ShapeDtypeStruct(features.shape, jnp.bfloat16),
            jax.ShapeDtypeStruct((LANES, 3 * LANES), jnp.float32),
        ),
        in_specs=[SMEM_SPEC] + [VMEM_SPEC] * 4,
        out_specs=(VMEM_SPEC,) * 2,
        scratch_shapes=[
            buffer(CHUNK, LANES),
            buffer(spatial, capacity, channels // spatial, voxels),
            wide(group, voxels, LANES),
            scalars(live, 27),
            scalars(live),
            scalars(group + 1),
            scalars(live),
            scalars(group),
            scalars(group),
            buffer(2, 4, 4, CHUNK, LANES),
            buffer(spatial, *block),
            buffer(spatial, capacity, channels // spatial, voxels),
            wide(live + 1, 64, 8, channels),
            buffer(9, live, 10, 64, channels),
            buffer(channels // spatial, live * voxels),
            wide(27 * channels + 16, LANES),
            buffer(27 * channels, LANES),
            buffer(channels // spatial, 27 * channels),
            wide(live + 1, 64, 8, LANES),
        ]
        + ring(4, CUT)
        + ring(4, rest)
        + [buffer(2, 4, CUT, LANES), buffer(2, 4, rest, LANES)]
        + ring(CUT)
        + ring(rest)
        + [
            buffer(2, CHUNK, LANES),
            buffer(CHUNK, LANES),
            buffer(live, 2, half, channels),
            buffer(live, half, channels),
            wide(live + 1, half, channels),
            buffer(live, half, channels),
            buffer(live + 1, half, channels),
            buffer(capacity, half, channels),
            buffer(capacity, half, channels),
            pltpu.SemaphoreType.DMA((2,)),
            pltpu.SemaphoreType.DMA((copies,)),
            pltpu.SemaphoreType.DMA((copies,)),
        ],
        compiler_params=pltpu.CompilerParams(
            collective_id=0, has_side_effects=True, vmem_limit_bytes=VMEM_BYTES
        ),
        cost_estimate=pl.CostEstimate(flops=flops, bytes_accessed=10**7, transcendentals=10**6),
    )(links, occupancy, features, cotangent, shard)


def body(features, cotangent, weight, occupancy, neighbours, first_moment, second_moment):
    input_grad, summed = step_call(neighbours, occupancy, features, cotangent, weight)
    scaled = summed[: first_moment.shape[1], : first_moment.shape[0]] / 64.0
    new_first = 0.9 * first_moment.T + 0.1 * scaled
    new_second = 0.999 * second_moment.T + 0.001 * scaled * scaled
    return input_grad, new_first.T, new_second.T


def solution(mesh):
    return jax.shard_map(
        body,
        mesh=mesh,
        in_specs=(
            P("dp", "space", None, None),
            P("dp", "space", None, None),
            P("dp", None),
            P("dp", None, None),
            P("dp", None, None),
            P("dp", "space"),
            P("dp", "space"),
        ),
        out_specs=(P("dp", "space", None, None), P("dp", "space"), P("dp", "space")),
        check_vma=False,
    )
```

```python
import jax
import jax.numpy as jnp
from jax import lax
from jax.experimental import pallas as pl
from jax.experimental.pallas import tpu as pltpu
from jax.sharding import PartitionSpec as P

LIVE = 4
LANES = 128
CHUNK = 336
CUT = 176
MESH = pl.DeviceIdType.MESH
VMEM_BYTES = 62 * 1024 * 1024


def fill_regions(table, blocks, regions, live):
    channels = blocks.shape[-1]
    row = lax.broadcasted_iota(jnp.int32, (1, 8, channels), 1)

    def plane(step, carry):
        r = step // 10
        i = step % 10
        first = jnp.where(i == 0, 0, jnp.where(i == 9, 2, 1))
        source = (i + 7) % 8
        code = 9 * first
        for c in range(3):
            pieces = []
            for second, start, count in ((0, 7, 1), (1, 0, 8), (2, 0, 1)):
                where = pl.ds(source * 8 + start, count)
                values = blocks[table[r, code + 3 * second + 1], where]
                if c != 1:
                    edge = blocks[table[r, code + 3 * second + c], where]
                    values = jnp.where(row == (7 if c == 0 else 0), edge, values)
                    values = pltpu.roll(values, 1 if c == 0 else 7, 1)
                pieces.append(values)
            line = jnp.concatenate(pieces, axis=0)
            for b in range(3):
                regions[3 * b + c, r, i] = (
                    line[b : b + 8].reshape(64, channels).astype(jnp.bfloat16)
                )
        return carry

    lax.fori_loop(0, live * 10, plane, 0)


def shifted_rows(regions, block, k, channels):
    a, bc = k // 9, k % 9
    return regions[bc, block, a : a + 8].reshape(512, channels)


SMEM_SPEC = pl.BlockSpec(memory_space=pltpu.SMEM)
VMEM_SPEC = pl.BlockSpec(memory_space=pltpu.VMEM)


class Wires:
    def __init__(self, send_sem, recv_sem):
        self.send_sem, self.recv_sem = send_sem, recv_sem
        dp, space = lax.axis_index("dp"), lax.axis_index("space")
        self.x, self.y, self.z = dp // 8, dp // 2 % 4, dp % 2
        self.chip, self.core = space // 2, space % 2
        self.started = []
        self.count = 0

    def at(self, x=None, y=None, z=None, chip=None, core=None):
        x, y, z = self.x if x is None else x, self.y if y is None else y, self.z if z is None else z
        chip, core = self.chip if chip is None else chip, self.core if core is None else core
        return (x * 8 + y * 2 + z, chip * 2 + core)

    def step(self, axis, by):
        return self.at(**{axis: (getattr(self, axis) + by) % 4})

    def greet(self, others):
        barrier = pltpu.get_barrier_semaphore()
        for other in others:
            pl.semaphore_signal(barrier, inc=1, device_id=other, device_id_type=MESH)

    def met(self, others):
        pl.semaphore_wait(pltpu.get_barrier_semaphore(), len(others))

    def everyone(self):
        return (
            [self.step(axis, by) for axis in ("x", "y") for by in (1, 3)]
            + [self.at(z=1 - self.z), self.at(chip=1 - self.chip), self.at(core=1 - self.core)]
            + [self.at(chip=1 - self.chip, core=1 - self.core)]
        )

    def ticket(self):
        self.count += 1
        return self.count - 1

    def send(self, ticket, source, target, other):
        copy = pltpu.make_async_remote_copy(
            source,
            target,
            self.send_sem.at[ticket],
            self.recv_sem.at[ticket],
            device_id=other,
            device_id_type=MESH,
        )
        copy.start()
        self.started.append(copy)

    def arrived(self, ticket, landing):
        pltpu.make_async_remote_copy(
            landing,
            landing,
            self.send_sem.at[ticket],
            self.recv_sem.at[ticket],
            device_id=self.at(core=1 - self.core),
            device_id_type=MESH,
        ).wait_recv()

    def finish(self):
        for copy in self.started:
            copy.wait_send()
        self.started = []


class RingGather:
    def __init__(self, wires, axis, block):
        self.wires, self.axis, self.block = wires, axis, block
        self.q = getattr(wires, axis)
        self.tickets = [wires.ticket() for _ in range(6)]

    def start(self):
        t, q = self.tickets, self.q
        right, left = self.wires.step(self.axis, 1), self.wires.step(self.axis, 3)
        for ticket, half, other in ((t[0], 0, right), (t[1], 1, left), (t[2], 1, right), (t[3], 0, left)):
            mine = self.block(q, half)
            self.wires.send(ticket, mine, mine, other)

    def forward(self):
        t, q = self.tickets, self.q
        right, left = self.wires.step(self.axis, 1), self.wires.step(self.axis, 3)
        for ticket, into, half, source, other in (
            (t[0], t[4], 0, (q + 3) % 4, right),
            (t[1], t[5], 1, (q + 1) % 4, left),
        ):
            piece = self.block(source, half)
            self.wires.arrived(ticket, piece)
            self.wires.send(into, piece, piece, other)

    def end(self):
        t, q = self.tickets, self.q
        self.wires.arrived(t[2], self.block((q + 3) % 4, 1))
        self.wires.arrived(t[3], self.block((q + 1) % 4, 0))
        self.wires.arrived(t[4], self.block((q + 2) % 4, 0))
        self.wires.arrived(t[5], self.block((q + 2) % 4, 1))


class RingReduce:
    def __init__(self, wires, axis, block, near, far_left, far_right):
        self.wires, self.axis, self.block = wires, axis, block
        self.near, self.far = near, (far_left, far_right)
        self.q = getattr(wires, axis)
        self.tickets = [wires.ticket() for _ in range(6)]

    def start(self):
        w, t, q = self.wires, self.tickets, self.q
        right, left = w.step(self.axis, 1), w.step(self.axis, 3)
        w.send(t[0], self.block((q + 2) % 4, 0), self.near.at[0], right)
        w.send(t[1], self.block((q + 2) % 4, 1), self.near.at[1], left)
        w.send(t[2], self.block((q + 1) % 4, 1), self.far[0].at[1], right)
        w.send(t[3], self.block((q + 3) % 4, 0), self.far[1].at[0], left)

    def forward(self):
        w, t, q = self.wires, self.tickets, self.q
        right, left = w.step(self.axis, 1), w.step(self.axis, 3)
        for half, target, other in ((0, (q + 1) % 4, right), (1, (q + 3) % 4, left)):
            w.arrived(t[half], self.near.at[half])
            own = self.block(target, half)[...].astype(jnp.float32)
            self.near[half] = (self.near[half].astype(jnp.float32) + own).astype(jnp.bfloat16)
            w.send(t[4 + half], self.near.at[half], self.far[half].at[half], other)

    def end(self, out):
        w, t, q = self.wires, self.tickets, self.q
        w.arrived(t[2], self.far[0].at[1])
        w.arrived(t[3], self.far[1].at[0])
        w.arrived(t[4], self.far[0].at[0])
        w.arrived(t[5], self.far[1].at[1])
        for half in range(2):
            total = self.block(q, half)[...].astype(jnp.float32)
            total = total + self.far[0][half].astype(jnp.float32)
            total = total + self.far[1][half].astype(jnp.float32)
            out[half] = total.astype(out.dtype)


def read_links(links, chip, table, slots, place, order, inward, onward):
    group = links.shape[1]
    alive = [(links[0, s, 13] >= 0).astype(jnp.int32) for s in range(group)]
    near = [(chip == s // (group // 2)).astype(jnp.int32) for s in range(group)]
    others = sum(a * (1 - n) for a, n in zip(alive, near))
    rank, counts, position = [], [0, 0], []
    total = 0
    for s in range(group):
        side = s // (group // 2)
        rank.append(total)
        position.append(counts[side] + near[s] * others)
        place[s + 1] = jnp.where(alive[s] > 0, jnp.minimum(total, LIVE), LIVE)
        inward[s] = jnp.where(alive[s] > 0, jnp.minimum(counts[side], LIVE), LIVE)
        onward[s] = jnp.where(alive[s] > 0, jnp.minimum(position[s], LIVE), LIVE)
        total = total + alive[s]
        counts[side] = counts[side] + alive[s]
    place[0] = LIVE
    for r in range(LIVE):
        slots[r] = sum(jnp.where(rank[s] == r, alive[s] * s, 0) for s in range(group))
        turn = sum(jnp.where(position[s] == r, alive[s] * rank[s], 0) for s in range(group))
        order[r] = jnp.minimum(turn, LIVE - 1)

    def code_of(code, carry):
        for r in range(LIVE):
            table[r, code] = place[links[0, slots[r], code] + 1]
        return carry

    lax.fori_loop(0, 27, code_of, 0)


def lanes_from(values, start):
    return pltpu.roll(values, (values.shape[1] - start) % values.shape[1], 1)[:, :LANES]


def step_kernel(
    links, occupancy, features, cotangent, shard, input_grad, grad,
    rows, cot_own, mask, table, slots, place, order, inward, onward,
    parts, feat, cot, blocks, regions, delta_t, stage, weight, weight_t, thin, pre_all,
    a_near, a_left, a_right, b_near, b_left, b_right, a_mid, b_mid,
    c_near, c_left, c_right, d_near, d_left, d_right, last, from_z,
    halves, inbox, chip_sum, z_out, z_in, fin_out, fin_in,
    local_sem, send_sem, recv_sem,
):
    live, group = LIVE, links.shape[1]
    capacity, voxels, channels = features.shape[1:]
    spatial = group // capacity
    width = channels // spatial
    rows_of = shard.shape[0]
    half = voxels // 2
    w = Wires(send_sem, recv_sem)
    x, y, z, chip, core = w.x, w.y, w.z, w.chip, w.core
    me, over, beside = chip * 2 + core, (1 - chip) * 2 + core, chip * 2 + 1 - core
    across = (1 - chip) * 2 + 1 - core
    to_over, to_beside = w.at(chip=1 - chip), w.at(core=1 - core)
    to_across = w.at(chip=1 - chip, core=1 - core)
    t_z, t_over, t_beside, t_across = (w.ticket() for _ in range(4))
    c_over, c_beside, c_across = (w.ticket() for _ in range(3))
    first_a = RingGather(w, "x", lambda q, h: parts.at[h, q, y, :CUT])
    first_b = RingGather(w, "y", lambda q, h: parts.at[h, x, q, CUT:])
    last_a = RingGather(w, "y", lambda q, h: parts.at[h, :, q, :CUT])
    last_b = RingGather(w, "x", lambda q, h: parts.at[h, q, :, CUT:])
    sum_a = RingReduce(w, "y", lambda q, h: parts.at[h, :, q, :CUT], a_near, a_left, a_right)
    sum_b = RingReduce(w, "x", lambda q, h: parts.at[h, q, :, CUT:], b_near, b_left, b_right)
    end_a = RingReduce(w, "x", lambda q, h: a_mid.at[h, q], c_near, c_left, c_right)
    end_b = RingReduce(w, "y", lambda q, h: b_mid.at[h, q], d_near, d_left, d_right)
    t_out, t_fin = w.ticket(), w.ticket()
    t_core = [w.ticket() for _ in range(live)]
    t_chip = [w.ticket() for _ in range(live)]

    w.greet(w.everyone())
    rows[CHUNK - 16 :] = jnp.zeros((16, LANES), jnp.bfloat16)
    start = (spatial - me) % spatial * width
    turned = pltpu.roll(shard[...].astype(jnp.float32), start, 1)[:, :LANES]
    lane = lax.broadcasted_iota(jnp.int32, turned.shape, 1)
    rows[:rows_of] = jnp.where(lane < width, turned, 0.0).astype(jnp.bfloat16)
    w.met(w.everyone())
    w.send(t_z, rows, parts.at[z, x, y], w.at(z=1 - z))
    w.send(t_over, features.at[0], feat.at[me], to_over)
    w.send(t_beside, features.at[0], feat.at[me], to_beside)
    keep = [
        pltpu.make_async_copy(rows, parts.at[z, x, y], local_sem.at[0]),
        pltpu.make_async_copy(features.at[0], feat.at[me], local_sem.at[1]),
    ]
    for copy in keep:
        copy.start()
    keep[0].wait()
    w.arrived(t_z, parts.at[1 - z, x, y])
    first_a.start()
    first_b.start()
    read_links(links, chip, table, slots, place, order, inward, onward)
    first_a.forward()
    first_b.forward()
    for s in range(spatial):
        for n in range(capacity):
            some = lanes_from(cotangent[0, n].astype(jnp.float32), s * width)
            cot_own[s, n] = some.T[:width].astype(jnp.bfloat16)
    cot[me] = cot_own[me]
    w.send(c_beside, cot_own.at[beside], cot.at[me], to_beside)
    first_a.end()
    first_b.end()
    last_a.start()
    last_b.start()
    held = occupancy[0].astype(jnp.float32)
    held = jnp.concatenate([held] * (LANES // group), axis=0).T
    for s in range(group):
        mask[s] = jnp.broadcast_to(held[:, s : s + 1], (voxels, LANES))
    w.arrived(t_over, feat.at[over])
    w.send(t_across, feat.at[over], feat.at[over], to_beside)
    w.send(c_over, cot_own.at[over], cot.at[me], to_over)
    w.send(c_across, cot_own.at[across], cot.at[me], to_across)
    last_a.forward()
    last_b.forward()
    keep[1].wait()
    w.arrived(t_beside, feat.at[beside])
    w.arrived(t_across, feat.at[across])

    for r in range(live):
        full = jnp.concatenate([mask[slots[r]]] * (channels // LANES), axis=1)
        field = feat[slots[r] // capacity, slots[r] % capacity].astype(jnp.float32)
        blocks[r] = (field * full).reshape(64, 8, channels)
    blocks[live] = jnp.zeros((64, 8, channels), jnp.float32)
    fill_regions(table, blocks, regions, live)
    last_a.end()
    last_b.end()
    for d in range(32):
        stage[rows_of * d : rows_of * d + CHUNK] = parts[d % 2, d // 8, d // 2 % 4].astype(
            jnp.float32
        )
    for k in range(27):
        some = stage[pl.ds(k, channels, stride=27), :]
        weight[k * channels : (k + 1) * channels] = some.astype(jnp.bfloat16)
        weight_t[:, k * channels : (k + 1) * channels] = some.T[:width].astype(jnp.bfloat16)

    def forward_block(r):
        pre = jnp.zeros((width, voxels), jnp.float32)
        for ks in (range(g, min(g + 2, 27)) for g in range(0, 27, 2)):
            field = jnp.concatenate([shifted_rows(regions, r, k, channels) for k in ks], axis=1)
            lhs = weight_t[:, ks[0] * channels : (ks[-1] + 1) * channels]
            pre = pre + lax.dot_general(
                lhs, field, (((1,), (1,)), ((), ())), preferred_element_type=jnp.float32
            )
        pre_all[r] = pre

    def delta_block(r):
        pre = pre_all[r]
        gate = jax.nn.sigmoid(pre)
        value = cot[slots[r] // capacity, slots[r] % capacity].astype(jnp.float32)
        value = value * occupancy[0, pl.ds(slots[r], 1)].astype(jnp.float32)
        value = (value * gate * (1.0 + pre * (1.0 - gate))).astype(jnp.bfloat16)
        delta_t[:, r * voxels : (r + 1) * voxels] = value
        value = jnp.concatenate(
            [value.astype(jnp.float32), jnp.zeros((LANES - width, voxels), jnp.float32)], axis=0
        )
        thin[r] = value.T.reshape(64, 8, LANES)

    for r in range(live):
        forward_block(r)
    w.arrived(c_over, cot.at[over])
    w.arrived(c_beside, cot.at[beside])
    w.arrived(c_across, cot.at[across])
    for r in range(live):
        delta_block(r)
    for k in range(27):
        field = jnp.concatenate(
            [shifted_rows(regions, r, k, channels) for r in range(live)], axis=0
        )
        part = jnp.dot(delta_t[...], field, preferred_element_type=jnp.float32)
        part = jnp.concatenate(
            [part, jnp.zeros((LANES - width, channels), jnp.float32)], axis=0
        )
        stage[pl.ds(k, channels, stride=27), :] = part.T
    w.finish()
    for d in range(32):
        parts[d % 2, d // 8, d // 2 % 4] = stage[rows_of * d : rows_of * d + CHUNK].astype(
            jnp.bfloat16
        )
    sum_a.start()
    sum_b.start()

    thin[live] = jnp.zeros((64, 8, LANES), jnp.float32)
    narrow = regions.at[:, :, :, :, :LANES]
    fill_regions(table, thin, narrow, live)

    chip_sum[live] = jnp.zeros((half, channels), jnp.float32)
    z_in[live] = jnp.zeros((half, channels), jnp.bfloat16)

    def back_block(j):
        r = order[j]
        out = jnp.zeros((voxels, channels), jnp.float32)
        for ks in (range(g, min(g + 4, 27)) for g in range(0, 27, 4)):
            lhs = jnp.concatenate([shifted_rows(narrow, r, 26 - k, LANES) for k in ks], axis=1)
            rhs = jnp.concatenate(
                [weight[k * channels : (k + 1) * channels] for k in ks], axis=1
            )
            out = out + lax.dot_general(
                lhs, rhs, (((1,), (1,)), ((), ())), preferred_element_type=jnp.float32
            )
        halves[j] = out.astype(jnp.bfloat16).reshape(2, half, channels)
        w.send(t_core[j], halves.at[j, 1 - core], inbox.at[j], to_beside)

    def join(j):
        w.arrived(t_core[j], inbox.at[j])
        value = halves[j, core].astype(jnp.float32) + inbox[j].astype(jnp.float32)
        chip_sum[j] = value
        z_out[j] = value.astype(jnp.bfloat16)
        w.send(t_chip[j], z_out.at[j], z_in.at[j], to_over)

    back_block(0)
    back_block(1)
    join(0)
    sum_a.forward()
    sum_b.forward()
    back_block(2)
    join(1)
    back_block(3)
    join(2)
    sum_a.end(a_mid)
    sum_b.end(b_mid)
    end_a.start()
    end_b.start()
    join(3)
    end_a.forward()
    end_b.forward()
    end_a.end(last.at[:, :CUT])
    end_b.end(last.at[:, CUT:])
    w.send(t_out, last.at[1 - z], from_z, w.at(z=1 - z))
    for j in range(live):
        w.arrived(t_chip[j], z_in.at[j])

    def whole(owner, n):
        s = owner * capacity + n
        return z_in[inward[s]].astype(jnp.float32) + chip_sum[onward[s]]

    def finish(n, part, value):
        span = pl.ds(pl.multiple_of(part * half, half), half)
        full = jnp.concatenate([mask[me * capacity + n, span]] * (channels // LANES), axis=1)
        value = cotangent[0, n, span].astype(jnp.float32) + full * value
        input_grad[0, n, span] = value.astype(jnp.bfloat16)

    for n in range(capacity):
        fin_out[n] = whole(beside, n).astype(jnp.bfloat16)
    w.send(t_fin, fin_out, fin_in, to_beside)
    for n in range(capacity):
        finish(n, core, whole(me, n))
    w.arrived(t_out, from_z)
    done = last[z].astype(jnp.float32) + from_z[...].astype(jnp.float32)
    fill = jnp.zeros((grad.shape[1] - CHUNK, LANES), jnp.float32)
    grad[...] = jnp.concatenate([done, fill], axis=0).T
    w.arrived(t_fin, fin_in)
    for n in range(capacity):
        finish(n, 1 - core, fin_in[n].astype(jnp.float32))
    w.finish()


def step_call(links, occupancy, features, cotangent, shard):
    live, group = LIVE, links.shape[1]
    capacity, voxels, channels = features.shape[1:]
    spatial, half = group // capacity, voxels // 2
    rest = CHUNK - CUT
    copies = 8 * 6 + 9 + 2 * live

    def buffer(*shape):
        return pltpu.VMEM(shape, jnp.bfloat16)

    def wide(*shape):
        return pltpu.VMEM(shape, jnp.float32)

    def ring(*shape):
        return [buffer(2, *shape, LANES)] * 3

    def scalars(*shape):
        return pltpu.SMEM(shape, jnp.int32)

    block = (capacity, voxels, channels)
    flops = 3 * 2 * live * voxels * 27 * channels * LANES
    return pl.pallas_call(
        step_kernel,
        out_shape=(
            jax.ShapeDtypeStruct(features.shape, jnp.bfloat16),
            jax.ShapeDtypeStruct((LANES, 3 * LANES), jnp.float32),
        ),
        in_specs=[SMEM_SPEC] + [VMEM_SPEC] * 4,
        out_specs=(VMEM_SPEC,) * 2,
        scratch_shapes=[
            buffer(CHUNK, LANES),
            buffer(spatial, capacity, channels // spatial, voxels),
            wide(group, voxels, LANES),
            scalars(live, 27),
            scalars(live),
            scalars(group + 1),
            scalars(live),
            scalars(group),
            scalars(group),
            buffer(2, 4, 4, CHUNK, LANES),
            buffer(spatial, *block),
            buffer(spatial, capacity, channels // spatial, voxels),
            wide(live + 1, 64, 8, channels),
            buffer(9, live, 10, 64, channels),
            buffer(channels // spatial, live * voxels),
            wide(27 * channels + 16, LANES),
            buffer(27 * channels, LANES),
            buffer(channels // spatial, 27 * channels),
            wide(live + 1, 64, 8, LANES),
            wide(live, channels // spatial, voxels),
        ]
        + ring(4, CUT)
        + ring(4, rest)
        + [buffer(2, 4, CUT, LANES), buffer(2, 4, rest, LANES)]
        + ring(CUT)
        + ring(rest)
        + [
            buffer(2, CHUNK, LANES),
            buffer(CHUNK, LANES),
            buffer(live, 2, half, channels),
            buffer(live, half, channels),
            wide(live + 1, half, channels),
            buffer(live, half, channels),
            buffer(live + 1, half, channels),
            buffer(capacity, half, channels),
            buffer(capacity, half, channels),
            pltpu.SemaphoreType.DMA((2,)),
            pltpu.SemaphoreType.DMA((copies,)),
            pltpu.SemaphoreType.DMA((copies,)),
        ],
        compiler_params=pltpu.CompilerParams(
            collective_id=0, has_side_effects=True, vmem_limit_bytes=VMEM_BYTES
        ),
        cost_estimate=pl.CostEstimate(flops=flops, bytes_accessed=10**7, transcendentals=10**6),
    )(links, occupancy, features, cotangent, shard)


def body(features, cotangent, weight, occupancy, neighbours, first_moment, second_moment):
    input_grad, summed = step_call(neighbours, occupancy, features, cotangent, weight)
    scaled = summed[: first_moment.shape[1], : first_moment.shape[0]] / 64.0
    new_first = 0.9 * first_moment.T + 0.1 * scaled
    new_second = 0.999 * second_moment.T + 0.001 * scaled * scaled
    return input_grad, new_first.T, new_second.T


def solution(mesh):
    return jax.shard_map(
        body,
        mesh=mesh,
        in_specs=(
            P("dp", "space", None, None),
            P("dp", "space", None, None),
            P("dp", None),
            P("dp", None, None),
            P("dp", None, None),
            P("dp", "space"),
            P("dp", "space"),
        ),
        out_specs=(P("dp", "space", None, None), P("dp", "space"), P("dp", "space")),
        check_vma=False,
    )
```

```python
import jax
import jax.numpy as jnp
from jax import lax
from jax.experimental import pallas as pl
from jax.experimental.pallas import tpu as pltpu
from jax.sharding import PartitionSpec as P

LIVE = 4
LANES = 128
CHUNK = 336
CUT = 176
MESH = pl.DeviceIdType.MESH
VMEM_BYTES = 62 * 1024 * 1024


def fill_regions(table, blocks, regions, live):
    channels = blocks.shape[-1]
    row = lax.broadcasted_iota(jnp.int32, (1, 8, channels), 1)

    def plane(step, carry):
        r = step // 10
        i = step % 10
        first = jnp.where(i == 0, 0, jnp.where(i == 9, 2, 1))
        source = (i + 7) % 8
        code = 9 * first
        for c in range(3):
            pieces = []
            for second, start, count in ((0, 7, 1), (1, 0, 8), (2, 0, 1)):
                where = pl.ds(source * 8 + start, count)
                values = blocks[table[r, code + 3 * second + 1], where]
                if c != 1:
                    edge = blocks[table[r, code + 3 * second + c], where]
                    values = jnp.where(row == (7 if c == 0 else 0), edge, values)
                    values = pltpu.roll(values, 1 if c == 0 else 7, 1)
                pieces.append(values)
            line = jnp.concatenate(pieces, axis=0)
            for b in range(3):
                regions[3 * b + c, r, i] = (
                    line[b : b + 8].reshape(64, channels).astype(jnp.bfloat16)
                )
        return carry

    lax.fori_loop(0, live * 10, plane, 0)


def shifted_rows(regions, block, k, channels):
    a, bc = k // 9, k % 9
    return regions[bc, block, a : a + 8].reshape(512, channels)


SMEM_SPEC = pl.BlockSpec(memory_space=pltpu.SMEM)
VMEM_SPEC = pl.BlockSpec(memory_space=pltpu.VMEM)


class Wires:
    def __init__(self, send_sem, recv_sem):
        self.send_sem, self.recv_sem = send_sem, recv_sem
        dp, space = lax.axis_index("dp"), lax.axis_index("space")
        self.x, self.y, self.z = dp // 8, dp // 2 % 4, dp % 2
        self.chip, self.core = space // 2, space % 2
        self.started = []
        self.count = 0

    def at(self, x=None, y=None, z=None, chip=None, core=None):
        x, y, z = self.x if x is None else x, self.y if y is None else y, self.z if z is None else z
        chip, core = self.chip if chip is None else chip, self.core if core is None else core
        return (x * 8 + y * 2 + z, chip * 2 + core)

    def step(self, axis, by):
        return self.at(**{axis: (getattr(self, axis) + by) % 4})

    def greet(self, others):
        barrier = pltpu.get_barrier_semaphore()
        for other in others:
            pl.semaphore_signal(barrier, inc=1, device_id=other, device_id_type=MESH)

    def met(self, others):
        pl.semaphore_wait(pltpu.get_barrier_semaphore(), len(others))

    def everyone(self):
        return (
            [self.step(axis, by) for axis in ("x", "y") for by in (1, 3)]
            + [self.at(z=1 - self.z), self.at(chip=1 - self.chip), self.at(core=1 - self.core)]
            + [self.at(chip=1 - self.chip, core=1 - self.core)]
        )

    def ticket(self):
        self.count += 1
        return self.count - 1

    def send(self, ticket, source, target, other):
        copy = pltpu.make_async_remote_copy(
            source,
            target,
            self.send_sem.at[ticket],
            self.recv_sem.at[ticket],
            device_id=other,
            device_id_type=MESH,
        )
        copy.start()
        self.started.append(copy)

    def arrived(self, ticket, landing):
        pltpu.make_async_remote_copy(
            landing,
            landing,
            self.send_sem.at[ticket],
            self.recv_sem.at[ticket],
            device_id=self.at(core=1 - self.core),
            device_id_type=MESH,
        ).wait_recv()

    def finish(self):
        for copy in self.started:
            copy.wait_send()
        self.started = []


class RingGather:
    def __init__(self, wires, axis, block):
        self.wires, self.axis, self.block = wires, axis, block
        self.q = getattr(wires, axis)
        self.tickets = [wires.ticket() for _ in range(6)]

    def start(self):
        t, q = self.tickets, self.q
        right, left = self.wires.step(self.axis, 1), self.wires.step(self.axis, 3)
        for ticket, half, other in ((t[0], 0, right), (t[1], 1, left), (t[2], 1, right), (t[3], 0, left)):
            mine = self.block(q, half)
            self.wires.send(ticket, mine, mine, other)

    def forward(self):
        t, q = self.tickets, self.q
        right, left = self.wires.step(self.axis, 1), self.wires.step(self.axis, 3)
        for ticket, into, half, source, other in (
            (t[0], t[4], 0, (q + 3) % 4, right),
            (t[1], t[5], 1, (q + 1) % 4, left),
        ):
            piece = self.block(source, half)
            self.wires.arrived(ticket, piece)
            self.wires.send(into, piece, piece, other)

    def end(self):
        t, q = self.tickets, self.q
        self.wires.arrived(t[2], self.block((q + 3) % 4, 1))
        self.wires.arrived(t[3], self.block((q + 1) % 4, 0))
        self.wires.arrived(t[4], self.block((q + 2) % 4, 0))
        self.wires.arrived(t[5], self.block((q + 2) % 4, 1))


class RingReduce:
    def __init__(self, wires, axis, block, near, far_left, far_right):
        self.wires, self.axis, self.block = wires, axis, block
        self.near, self.far = near, (far_left, far_right)
        self.q = getattr(wires, axis)
        self.tickets = [wires.ticket() for _ in range(6)]

    def start(self):
        w, t, q = self.wires, self.tickets, self.q
        right, left = w.step(self.axis, 1), w.step(self.axis, 3)
        w.send(t[0], self.block((q + 2) % 4, 0), self.near.at[0], right)
        w.send(t[1], self.block((q + 2) % 4, 1), self.near.at[1], left)
        w.send(t[2], self.block((q + 1) % 4, 1), self.far[0].at[1], right)
        w.send(t[3], self.block((q + 3) % 4, 0), self.far[1].at[0], left)

    def forward(self):
        w, t, q = self.wires, self.tickets, self.q
        right, left = w.step(self.axis, 1), w.step(self.axis, 3)
        for half, target, other in ((0, (q + 1) % 4, right), (1, (q + 3) % 4, left)):
            w.arrived(t[half], self.near.at[half])
            own = self.block(target, half)[...].astype(jnp.float32)
            self.near[half] = (self.near[half].astype(jnp.float32) + own).astype(jnp.bfloat16)
            w.send(t[4 + half], self.near.at[half], self.far[half].at[half], other)

    def end(self, out):
        w, t, q = self.wires, self.tickets, self.q
        w.arrived(t[2], self.far[0].at[1])
        w.arrived(t[3], self.far[1].at[0])
        w.arrived(t[4], self.far[0].at[0])
        w.arrived(t[5], self.far[1].at[1])
        for half in range(2):
            total = self.block(q, half)[...].astype(jnp.float32)
            total = total + self.far[0][half].astype(jnp.float32)
            total = total + self.far[1][half].astype(jnp.float32)
            out[half] = total.astype(out.dtype)


def read_links(links, chip, table, slots, place, order, inward, onward):
    group = links.shape[1]
    alive = [(links[0, s, 13] >= 0).astype(jnp.int32) for s in range(group)]
    near = [(chip == s // (group // 2)).astype(jnp.int32) for s in range(group)]
    others = sum(a * (1 - n) for a, n in zip(alive, near))
    rank, counts, position = [], [0, 0], []
    total = 0
    for s in range(group):
        side = s // (group // 2)
        rank.append(total)
        position.append(counts[side] + near[s] * others)
        place[s + 1] = jnp.where(alive[s] > 0, jnp.minimum(total, LIVE), LIVE)
        inward[s] = jnp.where(alive[s] > 0, jnp.minimum(counts[side], LIVE), LIVE)
        onward[s] = jnp.where(alive[s] > 0, jnp.minimum(position[s], LIVE), LIVE)
        total = total + alive[s]
        counts[side] = counts[side] + alive[s]
    place[0] = LIVE
    for r in range(LIVE):
        slots[r] = sum(jnp.where(rank[s] == r, alive[s] * s, 0) for s in range(group))
        turn = sum(jnp.where(position[s] == r, alive[s] * rank[s], 0) for s in range(group))
        order[r] = jnp.minimum(turn, LIVE - 1)

    def code_of(code, carry):
        for r in range(LIVE):
            table[r, code] = place[links[0, slots[r], code] + 1]
        return carry

    lax.fori_loop(0, 27, code_of, 0)


def lanes_from(values, start):
    return pltpu.roll(values, (values.shape[1] - start) % values.shape[1], 1)[:, :LANES]


def step_kernel(
    links, occupancy, features, cotangent, shard, input_grad, grad,
    rows, cot_own, mask, table, slots, place, order, inward, onward,
    parts, feat, cot, blocks, regions, delta_t, stage, weight, weight_t, thin, pre_all,
    a_near, a_left, a_right, b_near, b_left, b_right, a_mid, b_mid,
    c_near, c_left, c_right, d_near, d_left, d_right, last, from_z,
    halves, inbox, chip_sum, z_out, z_in, fin_out, fin_in,
    local_sem, send_sem, recv_sem,
):
    live, group = LIVE, links.shape[1]
    capacity, voxels, channels = features.shape[1:]
    spatial = group // capacity
    width = channels // spatial
    rows_of = shard.shape[0]
    half = voxels // 2
    w = Wires(send_sem, recv_sem)
    x, y, z, chip, core = w.x, w.y, w.z, w.chip, w.core
    me, over, beside = chip * 2 + core, (1 - chip) * 2 + core, chip * 2 + 1 - core
    across = (1 - chip) * 2 + 1 - core
    to_over, to_beside = w.at(chip=1 - chip), w.at(core=1 - core)
    to_across = w.at(chip=1 - chip, core=1 - core)
    t_z, t_beside = w.ticket(), w.ticket()
    t_over = [w.ticket() for _ in range(capacity)]
    t_across = [w.ticket() for _ in range(capacity)]
    c_over, c_beside, c_across = (w.ticket() for _ in range(3))
    first_a = RingGather(w, "x", lambda q, h: parts.at[h, q, y, :CUT])
    first_b = RingGather(w, "y", lambda q, h: parts.at[h, x, q, CUT:])
    last_a = RingGather(w, "y", lambda q, h: parts.at[h, :, q, :CUT])
    last_b = RingGather(w, "x", lambda q, h: parts.at[h, q, :, CUT:])
    sum_a = RingReduce(w, "y", lambda q, h: parts.at[h, :, q, :CUT], a_near, a_left, a_right)
    sum_b = RingReduce(w, "x", lambda q, h: parts.at[h, q, :, CUT:], b_near, b_left, b_right)
    end_a = RingReduce(w, "x", lambda q, h: a_mid.at[h, q], c_near, c_left, c_right)
    end_b = RingReduce(w, "y", lambda q, h: b_mid.at[h, q], d_near, d_left, d_right)
    t_out, t_fin = w.ticket(), w.ticket()
    t_core = [w.ticket() for _ in range(live)]
    t_chip = [w.ticket() for _ in range(live)]

    w.greet(w.everyone())
    rows[CHUNK - 16 :] = jnp.zeros((16, LANES), jnp.bfloat16)
    start = (spatial - me) % spatial * width
    turned = pltpu.roll(shard[...].astype(jnp.float32), start, 1)[:, :LANES]
    lane = lax.broadcasted_iota(jnp.int32, turned.shape, 1)
    rows[:rows_of] = jnp.where(lane < width, turned, 0.0).astype(jnp.bfloat16)
    w.met(w.everyone())
    w.send(t_z, rows, parts.at[z, x, y], w.at(z=1 - z))
    for n in range(capacity):
        w.send(t_over[n], features.at[0, n], feat.at[me, n], to_over)
    w.send(t_beside, features.at[0], feat.at[me], to_beside)
    keep = [
        pltpu.make_async_copy(rows, parts.at[z, x, y], local_sem.at[0]),
        pltpu.make_async_copy(features.at[0], feat.at[me], local_sem.at[1]),
    ]
    for copy in keep:
        copy.start()
    keep[0].wait()
    w.arrived(t_z, parts.at[1 - z, x, y])
    first_a.start()
    first_b.start()
    read_links(links, chip, table, slots, place, order, inward, onward)
    first_a.forward()
    first_b.forward()
    first_a.end()
    first_b.end()
    last_a.start()
    last_b.start()
    for s in range(spatial):
        for n in range(capacity):
            some = lanes_from(cotangent[0, n].astype(jnp.float32), s * width)
            cot_own[s, n] = some.T[:width].astype(jnp.bfloat16)
    cot[me] = cot_own[me]
    w.send(c_beside, cot_own.at[beside], cot.at[me], to_beside)
    for n in range(capacity):
        w.arrived(t_over[n], feat.at[over, n])
        w.send(t_across[n], feat.at[over, n], feat.at[over, n], to_beside)
    w.send(c_over, cot_own.at[over], cot.at[me], to_over)
    w.send(c_across, cot_own.at[across], cot.at[me], to_across)
    last_a.forward()
    last_b.forward()
    held = occupancy[0].astype(jnp.float32)
    held = jnp.concatenate([held] * (LANES // group), axis=0).T
    for s in range(group):
        mask[s] = jnp.broadcast_to(held[:, s : s + 1], (voxels, LANES))
    keep[1].wait()
    w.arrived(t_beside, feat.at[beside])
    for n in range(capacity):
        w.arrived(t_across[n], feat.at[across, n])

    for r in range(live):
        full = jnp.concatenate([mask[slots[r]]] * (channels // LANES), axis=1)
        field = feat[slots[r] // capacity, slots[r] % capacity].astype(jnp.float32)
        blocks[r] = (field * full).reshape(64, 8, channels)
    blocks[live] = jnp.zeros((64, 8, channels), jnp.float32)
    fill_regions(table, blocks, regions, live)
    last_a.end()
    last_b.end()
    for d in range(32):
        stage[rows_of * d : rows_of * d + CHUNK] = parts[d % 2, d // 8, d // 2 % 4].astype(
            jnp.float32
        )
    for k in range(27):
        some = stage[pl.ds(k, channels, stride=27), :]
        weight[k * channels : (k + 1) * channels] = some.astype(jnp.bfloat16)
        weight_t[:, k * channels : (k + 1) * channels] = some.T[:width].astype(jnp.bfloat16)

    def forward_block(r):
        pre = jnp.zeros((width, voxels), jnp.float32)
        for ks in (range(g, min(g + 2, 27)) for g in range(0, 27, 2)):
            field = jnp.concatenate([shifted_rows(regions, r, k, channels) for k in ks], axis=1)
            lhs = weight_t[:, ks[0] * channels : (ks[-1] + 1) * channels]
            pre = pre + lax.dot_general(
                lhs, field, (((1,), (1,)), ((), ())), preferred_element_type=jnp.float32
            )
        pre_all[r] = pre

    def delta_block(r):
        pre = pre_all[r]
        gate = jax.nn.sigmoid(pre)
        value = cot[slots[r] // capacity, slots[r] % capacity].astype(jnp.float32)
        value = value * occupancy[0, pl.ds(slots[r], 1)].astype(jnp.float32)
        value = (value * gate * (1.0 + pre * (1.0 - gate))).astype(jnp.bfloat16)
        delta_t[:, r * voxels : (r + 1) * voxels] = value
        value = jnp.concatenate(
            [value.astype(jnp.float32), jnp.zeros((LANES - width, voxels), jnp.float32)], axis=0
        )
        thin[r] = value.T.reshape(64, 8, LANES)

    for r in range(live):
        forward_block(r)
    w.arrived(c_over, cot.at[over])
    w.arrived(c_beside, cot.at[beside])
    w.arrived(c_across, cot.at[across])
    for r in range(live):
        delta_block(r)
    for k in range(27):
        field = jnp.concatenate(
            [shifted_rows(regions, r, k, channels) for r in range(live)], axis=0
        )
        part = jnp.dot(delta_t[...], field, preferred_element_type=jnp.float32)
        part = jnp.concatenate(
            [part, jnp.zeros((LANES - width, channels), jnp.float32)], axis=0
        )
        stage[pl.ds(k, channels, stride=27), :] = part.T
    w.finish()
    for ring, low, high in ((sum_a, 0, CUT), (sum_b, CUT, CHUNK)):
        for d in range(32):
            piece = stage[rows_of * d + low : rows_of * d + high]
            parts[d % 2, d // 8, d // 2 % 4, low:high] = piece.astype(jnp.bfloat16)
        ring.start()

    thin[live] = jnp.zeros((64, 8, LANES), jnp.float32)
    narrow = regions.at[:, :, :, :, :LANES]
    fill_regions(table, thin, narrow, live)

    chip_sum[live] = jnp.zeros((half, channels), jnp.float32)
    z_in[live] = jnp.zeros((half, channels), jnp.bfloat16)

    def back_block(j):
        r = order[j]
        out = jnp.zeros((voxels, channels), jnp.float32)
        for ks in (range(g, min(g + 4, 27)) for g in range(0, 27, 4)):
            lhs = jnp.concatenate([shifted_rows(narrow, r, 26 - k, LANES) for k in ks], axis=1)
            rhs = jnp.concatenate(
                [weight[k * channels : (k + 1) * channels] for k in ks], axis=1
            )
            out = out + lax.dot_general(
                lhs, rhs, (((1,), (1,)), ((), ())), preferred_element_type=jnp.float32
            )
        halves[j] = out.astype(jnp.bfloat16).reshape(2, half, channels)
        w.send(t_core[j], halves.at[j, 1 - core], inbox.at[j], to_beside)

    def join(j):
        w.arrived(t_core[j], inbox.at[j])
        value = halves[j, core].astype(jnp.float32) + inbox[j].astype(jnp.float32)
        chip_sum[j] = value
        z_out[j] = value.astype(jnp.bfloat16)
        w.send(t_chip[j], z_out.at[j], z_in.at[j], to_over)

    back_block(0)
    back_block(1)
    join(0)
    sum_a.forward()
    sum_b.forward()
    back_block(2)
    join(1)
    back_block(3)
    join(2)
    sum_a.end(a_mid)
    sum_b.end(b_mid)
    end_a.start()
    end_b.start()
    join(3)
    end_a.forward()
    end_b.forward()
    end_a.end(last.at[:, :CUT])
    end_b.end(last.at[:, CUT:])
    w.send(t_out, last.at[1 - z], from_z, w.at(z=1 - z))
    for j in range(live):
        w.arrived(t_chip[j], z_in.at[j])

    def whole(owner, n):
        s = owner * capacity + n
        return z_in[inward[s]].astype(jnp.float32) + chip_sum[onward[s]]

    def finish(n, part, value):
        span = pl.ds(pl.multiple_of(part * half, half), half)
        full = jnp.concatenate([mask[me * capacity + n, span]] * (channels // LANES), axis=1)
        value = cotangent[0, n, span].astype(jnp.float32) + full * value
        input_grad[0, n, span] = value.astype(jnp.bfloat16)

    for n in range(capacity):
        fin_out[n] = whole(beside, n).astype(jnp.bfloat16)
    w.send(t_fin, fin_out, fin_in, to_beside)
    for n in range(capacity):
        finish(n, core, whole(me, n))
    w.arrived(t_out, from_z)
    done = last[z].astype(jnp.float32) + from_z[...].astype(jnp.float32)
    fill = jnp.zeros((grad.shape[1] - CHUNK, LANES), jnp.float32)
    grad[...] = jnp.concatenate([done, fill], axis=0).T
    w.arrived(t_fin, fin_in)
    for n in range(capacity):
        finish(n, 1 - core, fin_in[n].astype(jnp.float32))
    w.finish()


def step_call(links, occupancy, features, cotangent, shard):
    live, group = LIVE, links.shape[1]
    capacity, voxels, channels = features.shape[1:]
    spatial, half = group // capacity, voxels // 2
    rest = CHUNK - CUT
    copies = 8 * 6 + 7 + 2 * capacity + 2 * live

    def buffer(*shape):
        return pltpu.VMEM(shape, jnp.bfloat16)

    def wide(*shape):
        return pltpu.VMEM(shape, jnp.float32)

    def ring(*shape):
        return [buffer(2, *shape, LANES)] * 3

    def scalars(*shape):
        return pltpu.SMEM(shape, jnp.int32)

    block = (capacity, voxels, channels)
    flops = 3 * 2 * live * voxels * 27 * channels * LANES
    return pl.pallas_call(
        step_kernel,
        out_shape=(
            jax.ShapeDtypeStruct(features.shape, jnp.bfloat16),
            jax.ShapeDtypeStruct((LANES, 3 * LANES), jnp.float32),
        ),
        in_specs=[SMEM_SPEC] + [VMEM_SPEC] * 4,
        out_specs=(VMEM_SPEC,) * 2,
        scratch_shapes=[
            buffer(CHUNK, LANES),
            buffer(spatial, capacity, channels // spatial, voxels),
            wide(group, voxels, LANES),
            scalars(live, 27),
            scalars(live),
            scalars(group + 1),
            scalars(live),
            scalars(group),
            scalars(group),
            buffer(2, 4, 4, CHUNK, LANES),
            buffer(spatial, *block),
            buffer(spatial, capacity, channels // spatial, voxels),
            wide(live + 1, 64, 8, channels),
            buffer(9, live, 10, 64, channels),
            buffer(channels // spatial, live * voxels),
            wide(27 * channels + 16, LANES),
            buffer(27 * channels, LANES),
            buffer(channels // spatial, 27 * channels),
            wide(live + 1, 64, 8, LANES),
            wide(live, channels // spatial, voxels),
        ]
        + ring(4, CUT)
        + ring(4, rest)
        + [buffer(2, 4, CUT, LANES), buffer(2, 4, rest, LANES)]
        + ring(CUT)
        + ring(rest)
        + [
            buffer(2, CHUNK, LANES),
            buffer(CHUNK, LANES),
            buffer(live, 2, half, channels),
            buffer(live, half, channels),
            wide(live + 1, half, channels),
            buffer(live, half, channels),
            buffer(live + 1, half, channels),
            buffer(capacity, half, channels),
            buffer(capacity, half, channels),
            pltpu.SemaphoreType.DMA((2,)),
            pltpu.SemaphoreType.DMA((copies,)),
            pltpu.SemaphoreType.DMA((copies,)),
        ],
        compiler_params=pltpu.CompilerParams(
            collective_id=0, has_side_effects=True, vmem_limit_bytes=VMEM_BYTES
        ),
        cost_estimate=pl.CostEstimate(flops=flops, bytes_accessed=10**7, transcendentals=10**6),
    )(links, occupancy, features, cotangent, shard)


def body(features, cotangent, weight, occupancy, neighbours, first_moment, second_moment):
    input_grad, summed = step_call(neighbours, occupancy, features, cotangent, weight)
    scaled = summed[: first_moment.shape[1], : first_moment.shape[0]] / 64.0
    new_first = 0.9 * first_moment.T + 0.1 * scaled
    new_second = 0.999 * second_moment.T + 0.001 * scaled * scaled
    return input_grad, new_first.T, new_second.T


def solution(mesh):
    return jax.shard_map(
        body,
        mesh=mesh,
        in_specs=(
            P("dp", "space", None, None),
            P("dp", "space", None, None),
            P("dp", None),
            P("dp", None, None),
            P("dp", None, None),
            P("dp", "space"),
            P("dp", "space"),
        ),
        out_specs=(P("dp", "space", None, None), P("dp", "space"), P("dp", "space")),
        check_vma=False,
    )
```
